256 devices in a mesh: dp: 16 (over z, y_hi), tensor: 16 (over y_lo, x, core).
Axes of the slice: x: 4, y: 4 (y_hi: 2, y_lo: 2; y = y_hi * 2 + y_lo), z: 8, core: 2. Of those that a mesh axis runs over, the one named last changes fastest.
Arguments:
- inputs: bfloat16 [112, 16, 256, 128], P('tensor', 'dp'), may hold values from -6 to 6
- cotangent: bfloat16 [112, 16, 256, 128], P('tensor', 'dp'), may hold values from -6 to 6
- w_expand: bfloat16 [256, 1024], P('dp', 'tensor'), may hold values from -0.375 to 0.375
- w_project: bfloat16 [256, 1024], P('dp', 'tensor'), may hold values from -0.375 to 0.375
- dw_kernel: bfloat16 [1024, 9], P('tensor'), may hold values from -2 to 2
- se_down: bfloat16 [64, 1024], P(None, 'tensor'), may hold values from -0.75 to 0.75
- se_up: bfloat16 [64, 1024], P(None, 'tensor'), may hold values from -1.5 to 1.5
Outputs:
- block_out: bfloat16 [112, 16, 256, 128], P('tensor', 'dp')
- input_grad: bfloat16 [112, 16, 256, 128], P('tensor', 'dp')
- expand_grad: float32 [256, 1024], P('dp', 'tensor')
- project_grad: float32 [256, 1024], P('dp', 'tensor')
- kernel_grad: float32 [1024, 9], P('tensor')
- down_grad: float32 [64, 1024], P(None, 'tensor')
- up_grad: float32 [64, 1024], P(None, 'tensor')
The draws below stay inside these ranges and needn't reach their ends.
All inputs are finite; a program needn't handle non-finite values.
Results may differ from the reference program's by a relative error of at most 0.025.
Values may be sent and summed in bfloat16 or wider, within the bound.
No kernel may reach another device: no remote copies, remote signals or barrier semaphores. Data moves between devices by JAX's collectives and lax.ppermute only.
A program may use at most 128 MiB of HBM per device.

```python
import jax
import jax.numpy as jnp
from jax import lax

C = 256
E = 1024
S = 64
H = 112
W = 128
IMAGES = 16
N_TENSOR = 16


def block_levels(stream_key, dims, shards, low, top_value):
    loudness = 1.0
    for dim, parts in shards:
        steps = jax.random.uniform(jax.random.fold_in(jax.random.fold_in(stream_key, 6), dim), (parts,), jnp.float32, low / len(shards), top_value / len(shards))
        loudness = loudness * jnp.repeat(jnp.exp(steps), dims[dim] // parts).reshape((-1,) + (1,) * (len(dims) - 1 - dim))
    return loudness


def centred(key, shape, deviation, bound, shards=(), kind=jnp.bfloat16):
    values = deviation * jax.random.normal(key, shape, jnp.float32)
    if shards:
        values = values * block_levels(key, shape, shards, -0.22, 0.18)
    return jnp.clip(values, -bound, bound).astype(kind)


def setup_inputs(seed: int = 0) -> dict:
    key_list = jax.random.split(jax.random.key(seed), 8)
    return {
        "inputs": centred(key_list[0], (H, IMAGES, C, W), 1.0, 6.0, ((0, 16), (1, 16))),
        "cotangent": centred(key_list[1], (H, IMAGES, C, W), 1.0, 6.0, ((0, 16), (1, 16))),
        "w_expand": centred(key_list[2], (C, E), C ** -0.5, 0.375, ((0, 16), (1, 16))),
        "w_project": centred(key_list[3], (C, E), C ** -0.5, 0.375, ((0, 16), (1, 16))),
        "dw_kernel": centred(key_list[4], (E, 9), 9 ** -0.5, 2.0, ((0, 16),)),
        "se_down": centred(key_list[5], (S, E), (E // 16) ** -0.5, 0.75, ((1, 16),)),
        "se_up": centred(key_list[6], (S, E), (S // 4) ** -0.5, 1.5, ((1, 16),)),
    }


gelu_scale = 0.7978845608
gelu_cubic = 0.044715

def gelu_pair(values):
    inner = gelu_scale * (values + gelu_cubic * values * values * values)
    tanh_part = jnp.tanh(inner)
    result = 0.5 * values * (1.0 + tanh_part)
    slope = 0.5 * (1.0 + tanh_part) + 0.5 * values * (1.0 - tanh_part * tanh_part) * gelu_scale * (1.0 + 3.0 * gelu_cubic * values * values)
    return (result, slope)

def shifted(source, shift_down, shift_right):
    height = source.shape[0]
    col_count = source.shape[3]
    padded = jnp.pad(source, ((1, 1), (0, 0), (0, 0), (1, 1)))
    return padded[1 + shift_down:1 + shift_down + height, :, :, 1 + shift_right:1 + shift_right + col_count]

def depthwise(source, kernel):
    running = jnp.zeros_like(source)
    for tap_index in range(9):
        running = running + kernel[:, tap_index][None, None, :, None] * shifted(source, tap_index // 3 - 1, tap_index % 3 - 1)
    return running

def depthwise_back(grad_out, source, kernel):
    grad_in = jnp.zeros_like(grad_out)
    tap_sums = []
    for tap_index in range(9):
        shift_down = tap_index // 3 - 1
        shift_right = tap_index % 3 - 1
        grad_in = grad_in + kernel[:, tap_index][None, None, :, None] * shifted(grad_out, -shift_down, -shift_right)
        tap_sums.append(lax.optimization_barrier(jnp.sum(grad_out * shifted(source, shift_down, shift_right), axis=(0, 1, 3))))
    return (grad_in, jnp.stack(tap_sums, axis=1))

def layer_norm(image):
    values = image.astype(jnp.float32)
    center = values - lax.optimization_barrier(jnp.mean(values, axis=2, keepdims=True))
    inv_std = lax.rsqrt(lax.optimization_barrier(jnp.mean(center * center, axis=2, keepdims=True)) + 1e-05)
    return (center * inv_std, inv_std)

def grouped_sum(activation, weight, group_count):
    shape = activation.shape
    split_act = activation.astype(jnp.float32).reshape(shape[0], shape[1], group_count, shape[2] // group_count, shape[3])
    split_weight = weight.astype(jnp.float32).reshape(weight.shape[0], group_count, -1)
    group_terms = jnp.einsum('hbgew,cge->hbgcw', split_act, split_weight, precision=lax.Precision.HIGHEST)
    return lax.optimization_barrier(jnp.sum(lax.optimization_barrier(group_terms.astype(jnp.bfloat16)).astype(jnp.float32), axis=2))

def reference(inputs, cotangent, w_expand, w_project, dw_kernel, se_down, se_up):
    highest = lax.Precision.HIGHEST
    exp32 = w_expand.astype(jnp.float32)
    proj32 = w_project.astype(jnp.float32)
    kernel32 = dw_kernel.astype(jnp.float32)
    down32 = se_down.astype(jnp.float32)
    up_weight32 = se_up.astype(jnp.float32)

    def one_image(carry, pair):
        image = pair[0][:, None]
        grad_out = pair[1][:, None]
        normal32, inv_std = layer_norm(image)
        normed = normal32.astype(jnp.bfloat16)
        normed32 = normed.astype(jnp.float32)
        expanded = jnp.einsum('hbcw,ce->hbew', normed32, exp32, precision=highest).astype(jnp.bfloat16)
        act_one, slope_one = gelu_pair(expanded.astype(jnp.float32))
        mixed = depthwise(act_one, kernel32)
        act_two, slope_two = gelu_pair(mixed)
        pooled = lax.optimization_barrier(jnp.mean(act_two, axis=(0, 1, 3)))
        squeeze = jnp.dot(down32, pooled, precision=highest)
        sig_squeeze = jax.nn.sigmoid(squeeze)
        swish_value = squeeze * sig_squeeze
        gating = jax.nn.sigmoid(jnp.dot(swish_value, up_weight32, precision=highest))
        hidden = (act_two * gating[None, None, :, None]).astype(jnp.bfloat16)
        projected = grouped_sum(hidden, proj32, N_TENSOR)
        block_out = (image.astype(jnp.float32) + projected).astype(jnp.bfloat16)
        grad32 = grad_out.astype(jnp.float32)
        grad_hidden = jnp.einsum('hbcw,ce->hbew', grad32, proj32, precision=highest).astype(jnp.bfloat16)
        grad_h32 = grad_hidden.astype(jnp.float32)
        g_project = jnp.einsum('hbcw,hbew->ce', grad32, hidden.astype(jnp.float32), precision=highest)
        grad_gate = lax.optimization_barrier(jnp.sum(grad_h32 * act_two, axis=(0, 1, 3)))
        grad_excite = grad_gate * gating * (1.0 - gating)
        g_up = swish_value[:, None] * grad_excite[None, :]
        grad_swish = jnp.dot(up_weight32, grad_excite, precision=highest)
        grad_squeeze = grad_swish * sig_squeeze * (1.0 + squeeze * (1.0 - sig_squeeze))
        g_down = grad_squeeze[:, None] * pooled[None, :]
        grad_pooled = jnp.dot(grad_squeeze, down32, precision=highest)
        grad_act_two = grad_h32 * gating[None, None, :, None] + grad_pooled[None, None, :, None] / (H * W)
        grad_mixed = grad_act_two * slope_two
        grad_act_one, g_kernel = depthwise_back(grad_mixed, act_one, kernel32)
        grad_expanded = (grad_act_one * slope_one).astype(jnp.bfloat16)
        g_expand = jnp.einsum('hbcw,hbew->ce', normed32, grad_expanded.astype(jnp.float32), precision=highest)
        grad_normed = grouped_sum(grad_expanded, exp32, N_TENSOR)
        mean_grad = lax.optimization_barrier(jnp.mean(grad_normed, axis=2, keepdims=True))
        mean_inner = lax.optimization_barrier(jnp.mean(grad_normed * normal32, axis=2, keepdims=True))
        input_grad = (grad32 + inv_std * (grad_normed - mean_grad - normal32 * mean_inner)).astype(jnp.bfloat16)
        new_carry = (carry[0] + g_expand, carry[1] + g_project, carry[2] + g_kernel, carry[3] + g_down, carry[4] + g_up)
        return (new_carry, (block_out[:, 0], input_grad[:, 0]))
    start_carry = (jnp.zeros((C, E), jnp.float32), jnp.zeros((C, E), jnp.float32), jnp.zeros((E, 9), jnp.float32), jnp.zeros((S, E), jnp.float32), jnp.zeros((S, E), jnp.float32))
    final, stacked = lax.scan(one_image, start_carry, (jnp.moveaxis(inputs, 1, 0), jnp.moveaxis(cotangent, 1, 0)))
    block_out = jnp.moveaxis(stacked[0], 0, 1)
    input_grad = jnp.moveaxis(stacked[1], 0, 1)
    return (block_out, input_grad, final[0], final[1], final[2], final[3], final[4])
```

```python
import jax
import jax.numpy as jnp
from jax import lax
from jax.experimental import pallas as pl
from jax.experimental.pallas import tpu as pltpu
from jax.sharding import PartitionSpec as P

bf16 = jnp.bfloat16
f32 = jnp.float32

gelu_scale = 0.7978845608
gelu_cubic = 0.044715

CH = 256
HALF = 512
SQ = 64
COLS = 128
ROWS = 14
EXT = ROWS + 4
CELLS = 112 * 128
BLOCKS = 4
GROUP = 16
BOTH = ("dp", "tensor")
VMEM = 48 * 1024 * 1024


def groups(count, steps):
    seen, found = set(), []
    for first in range(count):
        if first in seen:
            continue
        members = [first]
        for step in steps:
            members = members + [member ^ step for member in members]
        members = sorted(members)
        seen.update(members)
        found.append(members)
    return found


def exchange(pieces, axes, steps=None):
    members = None
    if steps is not None:
        members = groups(256 if axes == BOTH else 16, steps)
    return lax.all_to_all(pieces, axes, 0, 0, tiled=True, axis_index_groups=members)


def to_all(piece, count):
    return jnp.broadcast_to(piece[None], (count,) + piece.shape)


PLANE = (2, 4, 8, 16)
DEPTH = (2, 4, 8)


def gelu_pair(values):
    square = values * values
    inner = values * (gelu_scale + (gelu_scale * gelu_cubic) * square)
    part = 0.5 + 0.5 * jnp.tanh(inner)
    act = values * part
    slope = part + act * (1.0 - part) * (
        2.0 * gelu_scale + (6.0 * gelu_scale * gelu_cubic) * square
    )
    return act, slope


def params(**more):
    return pltpu.CompilerParams(vmem_limit_bytes=VMEM, **more)


def cost(flops, size):
    return pl.CostEstimate(flops=flops, bytes_accessed=size, transcendentals=0)


def join_low(first, second, low):
    return jnp.where(low, first, pltpu.roll(second, 64, 1))


def join_high(first, second, low):
    return jnp.where(low, pltpu.roll(first, 64, 1), second)


def lanes_of(shape):
    return lax.broadcasted_iota(jnp.int32, shape, 1)


def down_rows(row):
    return jnp.broadcast_to(row, (128, 128)).T


def norm_kernel(pos, own_x, other_x, own_c, other_c, top, bottom, normed, cot):
    row = pl.program_id(0)
    pair_row = row - 2
    mine = (pair_row >= 7).astype(jnp.int32) == pos[0]
    x = jnp.where(mine, own_x[0, 0], other_x[0, 0])
    c = jnp.where(mine, own_c[0, 0], other_c[0, 0])
    x = jnp.where(row < 2, top[0, 0], jnp.where(row >= ROWS + 2, bottom[0, 0], x))
    c = jnp.where(row < 2, top[1, 0], jnp.where(row >= ROWS + 2, bottom[1, 0], c))
    values = x.astype(f32)
    center = values - jnp.mean(values, axis=0, keepdims=True)
    inv_std = lax.rsqrt(jnp.mean(center * center, axis=0, keepdims=True) + 1e-05)
    normed[...] = (center * inv_std).astype(bf16)
    cot[...] = c


def norm_rows(pos, own_x, other_x, own_c, other_c, top, bottom):
    def own_map(i, pos):
        return (jnp.clip(i - 2 - 7 * pos[0], 0, 6), 0, 0, 0)

    def other_map(i, pos):
        return (jnp.clip(i - 2 - 7 * (1 - pos[0]), 0, 6), 0, 0, 0)

    row_block = (1, 1, CH, COLS)
    return pl.pallas_call(
        norm_kernel,
        grid_spec=pltpu.PrefetchScalarGridSpec(
            num_scalar_prefetch=1,
            grid=(EXT,),
            in_specs=[
                pl.BlockSpec(row_block, own_map),
                pl.BlockSpec(row_block, other_map),
                pl.BlockSpec(row_block, own_map),
                pl.BlockSpec(row_block, other_map),
                pl.BlockSpec((2, 1, CH, COLS), lambda i, pos: (0, jnp.clip(i, 0, 1), 0, 0)),
                pl.BlockSpec(
                    (2, 1, CH, COLS), lambda i, pos: (0, jnp.clip(i - ROWS - 2, 0, 1), 0, 0)
                ),
            ],
            out_specs=[
                pl.BlockSpec((CH, COLS), lambda i, pos: (0, i)),
                pl.BlockSpec((CH, COLS), lambda i, pos: (0, i)),
            ],
        ),
        out_shape=[jax.ShapeDtypeStruct((CH, EXT * COLS), bf16)] * 2,
        compiler_params=params(),
        cost_estimate=cost(10**9, 8 * 10**6),
        name="norm_rows",
    )(pos, own_x, other_x, own_c, other_c, top, bottom)


def spread_taps(small, taps, masked):
    low = lanes_of((16, 128)) < 64
    first = small[0, 0, 64:80, :].astype(f32)
    second = small[1, 0, 64:80, :].astype(f32)
    rows = join_low(first, second, low)
    lane = lanes_of((128, 128))
    for tap in range(9):
        spread = down_rows(rows[tap : tap + 1, :])
        if masked and tap % 3 == 0:
            spread = jnp.where(lane == 0, 0.0, spread)
        if masked and tap % 3 == 2:
            spread = jnp.where(lane == 127, 0.0, spread)
        taps[tap] = spread


def forward_kernel(
    pos, weights, small, normed, cot,
    act1, slope1, act2, part_p, part_q, proj_grad, w_exp, w_proj, sums,
    expanded, grad_hidden, taps, pool, gate,
):
    step = pl.program_id(0)
    low = lanes_of((16, 128)) < 64
    for z in range(8):
        for yh in range(2):
            first = weights[yh, 0, z].astype(f32)
            second = weights[yh, 1, z].astype(f32)
            rows = pl.ds((z * 2 + yh) * 16, 16)
            w_exp[rows, :] = join_low(first, second, low).astype(bf16)
            w_proj[rows, :] = join_high(first, second, low).astype(bf16)
    spread_taps(small, taps, True)
    w_exp_t = w_exp[...].astype(f32).T.astype(bf16)
    w_proj_t = w_proj[...].astype(f32).T.astype(bf16)
    for part in range(EXT // 2):
        cells = slice(part * 256, part * 256 + 256)
        expanded[:, cells] = jnp.dot(
            w_exp_t, normed[:, cells], preferred_element_type=f32
        ).astype(bf16)
    for part in range(ROWS // 2 + 1):
        cells = slice(part * 256, part * 256 + 256)
        source = slice(part * 256 + 128, part * 256 + 384)
        grad_hidden[:, cells] = jnp.dot(
            w_proj_t, cot[:, source], preferred_element_type=f32
        ).astype(bf16)
    first_chip = pos[1].astype(f32)
    last_chip = pos[2].astype(f32)

    def one_group(index, carry):
        rows = pl.ds(pl.multiple_of(index * GROUP, GROUP), GROUP)
        tap = [taps[k, rows, :] for k in range(9)]
        running = {}
        pool_sum = jnp.zeros((GROUP, COLS), f32)
        gate_sum = jnp.zeros((GROUP, COLS), f32)
        for h in range(EXT):
            value = expanded[rows, h * 128 : h * 128 + 128].astype(f32)
            act, slope = gelu_pair(value)
            act1[rows, h * 128 : h * 128 + 128] = act.astype(bf16)
            if 2 <= h < ROWS + 2:
                slope1[rows, (h - 2) * 128 : (h - 1) * 128] = slope.astype(bf16)
            left = pltpu.roll(act, 1, 1)
            right = pltpu.roll(act, 127, 1)
            for i in range(3):
                m = h + 1 - i
                if not 1 <= m <= ROWS + 2:
                    continue
                term = tap[3 * i] * left + tap[3 * i + 1] * act + tap[3 * i + 2] * right
                running[m] = running[m] + term if m in running else term
            m = h - 1
            if not 1 <= m <= ROWS + 2:
                continue
            act, slope = gelu_pair(running.pop(m))
            grad = grad_hidden[rows, (m - 1) * 128 : m * 128].astype(f32)
            if m == 1:
                slope = slope * first_chip
            if m == ROWS + 2:
                slope = slope * last_chip
            part_q[rows, (m - 1) * 128 : m * 128] = slope.astype(bf16)
            part_p[rows, (m - 1) * 128 : m * 128] = (slope * grad).astype(bf16)
            if 2 <= m < ROWS + 2:
                act2[rows, (m - 2) * 128 : (m - 1) * 128] = act.astype(bf16)
                pool_sum = pool_sum + act
                gate_sum = gate_sum + act * grad
        pool[rows, :] = pool_sum
        gate[rows, :] = gate_sum
        return carry

    lax.fori_loop(0, 128 // GROUP, one_group, 0)
    sums[pl.ds(step, 1), :] = jnp.sum(pool[...].T, axis=0, keepdims=True)
    sums[pl.ds(step + BLOCKS, 1), :] = jnp.sum(gate[...].T, axis=0, keepdims=True)
    proj_grad[...] = lax.dot_general(
        cot[:, 256 : 256 + ROWS * COLS],
        act2[...],
        (((1,), (1,)), ((), ())),
        preferred_element_type=f32,
    )


def forward(pos, weights, small, normed, cot):
    def along(width):
        return pl.BlockSpec((128, width * COLS), lambda g, pos: (g, 0))

    across = pl.BlockSpec((CH, 128), lambda g, pos: (0, g))
    whole = pl.BlockSpec((CH, EXT * COLS), lambda g, pos: (0, 0))
    return pl.pallas_call(
        forward_kernel,
        grid_spec=pltpu.PrefetchScalarGridSpec(
            num_scalar_prefetch=1,
            grid=(BLOCKS,),
            in_specs=[
                pl.BlockSpec((2, 2, 8, 16, 128), lambda g, pos: (0, g, 0, 0, 0)),
                pl.BlockSpec((2, 1, 80, 128), lambda g, pos: (g, pos[0], 0, 0)),
                whole,
                whole,
            ],
            out_specs=[
                along(EXT),
                along(ROWS),
                along(ROWS),
                along(ROWS + 2),
                along(ROWS + 2),
                across,
                across,
                across,
                pl.BlockSpec((8, 128), lambda g, pos: (0, 0)),
            ],
            scratch_shapes=[
                pltpu.VMEM((128, EXT * COLS), bf16),
                pltpu.VMEM((128, (ROWS + 2) * COLS), bf16),
                pltpu.VMEM((9, 128, 128), f32),
                pltpu.VMEM((128, 128), f32),
                pltpu.VMEM((128, 128), f32),
            ],
        ),
        out_shape=[
            jax.ShapeDtypeStruct((HALF, EXT * COLS), bf16),
            jax.ShapeDtypeStruct((HALF, ROWS * COLS), bf16),
            jax.ShapeDtypeStruct((HALF, ROWS * COLS), bf16),
            jax.ShapeDtypeStruct((HALF, (ROWS + 2) * COLS), bf16),
            jax.ShapeDtypeStruct((HALF, (ROWS + 2) * COLS), bf16),
            jax.ShapeDtypeStruct((CH, HALF), f32),
            jax.ShapeDtypeStruct((CH, HALF), bf16),
            jax.ShapeDtypeStruct((CH, HALF), bf16),
            jax.ShapeDtypeStruct((8, 128), f32),
        ],
        compiler_params=params(),
        cost_estimate=cost(10**10, 40 * 10**6),
        name="forward",
    )(pos, weights, small, normed, cot)


def excite_kernel(pos, sums, small, coef, vectors, pooled_all, gate_all):
    low = lanes_of((SQ, 128)) < 64
    totals = []
    for core in range(2):
        total = sums[core]
        for other in range(1, 8):
            total = total + sums[2 * other + core]
        totals.append(total)
    pooled, grad_gate, down, up = [], [], [], []
    for core in range(2):
        for block in range(BLOCKS):
            pooled.append(totals[core][block : block + 1] * (1.0 / CELLS))
            grad_gate.append(totals[core][BLOCKS + block : BLOCKS + block + 1])
            first = small[4 * block + core, 0:SQ, :].astype(f32)
            second = small[4 * block + 2 + core, 0:SQ, :].astype(f32)
            down.append(join_low(first, second, low))
            up.append(join_high(first, second, low))
    count = 2 * BLOCKS
    squeeze = sum(jnp.sum(down[b] * pooled[b], axis=1, keepdims=True) for b in range(count))
    sig = 1.0 / (1.0 + jnp.exp(-squeeze))
    swish = squeeze * sig
    gating, grad_excite = [], []
    for b in range(count):
        logit = jnp.sum(up[b] * swish, axis=0, keepdims=True)
        gating.append(1.0 / (1.0 + jnp.exp(-logit)))
        grad_excite.append(grad_gate[b] * gating[b] * (1.0 - gating[b]))
    grad_swish = sum(jnp.sum(up[b] * grad_excite[b], axis=1, keepdims=True) for b in range(count))
    grad_squeeze = grad_swish * sig * (1.0 + squeeze * (1.0 - sig))
    for core in range(2):

        @pl.when(pos[0] == core)
        def _():
            for block in range(BLOCKS):
                b = core * BLOCKS + block
                cells = slice(block * 128, block * 128 + 128)
                grad_pooled = jnp.sum(down[b] * grad_squeeze, axis=0, keepdims=True)
                coef[0:1, cells] = gating[b]
                coef[1:2, cells] = grad_pooled * (1.0 / CELLS)
                pooled_all[block] = pooled[b]
                gate_all[block] = grad_excite[b]

    coef[2:8, :] = jnp.zeros((6, HALF), f32)
    place = pos[3]
    turned = lax.rem(place, 2) == 1
    block = lax.div(place, 2)
    own_pool = pooled_all[block]
    own_gate = gate_all[block]
    row_low = lanes_of((1, 128)) < 64
    side = jnp.concatenate([swish, grad_squeeze], axis=0)
    vectors[0:1, :] = jnp.broadcast_to(side, (128, 128)).T[0:1, :]
    vectors[1:2, :] = jnp.where(
        turned,
        jnp.where(row_low, pltpu.roll(own_pool, 64, 1), own_gate),
        jnp.where(row_low, own_pool, pltpu.roll(own_gate, 64, 1)),
    )
    vectors[2:8, :] = jnp.zeros((6, 128), f32)


def excite(pos, sums, small):
    return pl.pallas_call(
        excite_kernel,
        in_specs=[
            pl.BlockSpec(memory_space=pltpu.SMEM),
            pl.BlockSpec(memory_space=pltpu.VMEM),
            pl.BlockSpec(memory_space=pltpu.VMEM),
        ],
        out_specs=[pl.BlockSpec(memory_space=pltpu.VMEM)] * 2,
        out_shape=[
            jax.ShapeDtypeStruct((8, HALF), f32),
            jax.ShapeDtypeStruct((8, 128), f32),
        ],
        scratch_shapes=[
            pltpu.VMEM((BLOCKS, 1, 128), f32),
            pltpu.VMEM((BLOCKS, 1, 128), f32),
        ],
        compiler_params=params(),
        cost_estimate=cost(10**8, 2 * 10**6),
        name="excite",
    )(pos, sums, small)


def backward_kernel(
    pos, coef, small, normed, act1, slope1, part_p, part_q, proj_grad,
    grad_expanded, pieces,
    taps, gates, pools, kernel_sums, tap_rows,
):
    spread_taps(small, taps, False)
    gates[...] = down_rows(coef[0:1, :])
    pools[...] = down_rows(coef[1:2, :])
    lane = lanes_of((GROUP, COLS))

    def one_group(index, carry):
        rows = pl.ds(pl.multiple_of(index * GROUP, GROUP), GROUP)
        tap = [taps[k, rows, :] for k in range(9)]
        gating = gates[rows, :]
        pooled = pools[rows, :]
        running = {}
        sums = [None] * 9
        for m in range(1, ROWS + 3):
            cells = slice((m - 1) * 128, m * 128)
            grad = part_p[rows, cells].astype(f32) * gating + part_q[rows, cells].astype(f32) * pooled
            turned = (
                jnp.where(lane == 127, 0.0, pltpu.roll(grad, 127, 1)),
                grad,
                jnp.where(lane == 0, 0.0, pltpu.roll(grad, 1, 1)),
            )
            for i in range(3):
                h = m + i - 1
                if 2 <= h < ROWS + 2:
                    term = tap[3 * i] * turned[0] + tap[3 * i + 1] * turned[1] + tap[3 * i + 2] * turned[2]
                    running[h] = running[h] + term if h in running else term
                if 2 <= m < ROWS + 2:
                    act = act1[rows, h * 128 : h * 128 + 128].astype(f32)
                    for j in range(3):
                        term = turned[j] * act
                        k = 3 * i + j
                        sums[k] = term if sums[k] is None else sums[k] + term
            h = m - 1
            if 2 <= h < ROWS + 2:
                out = slice((h - 2) * 128, (h - 1) * 128)
                grad_expanded[rows, out] = (running.pop(h) * slope1[rows, out].astype(f32)).astype(bf16)
        for k in range(9):
            kernel_sums[k, rows, :] = sums[k]
        return carry

    lax.fori_loop(0, 128 // GROUP, one_group, 0)
    exp_grad = lax.dot_general(
        normed[:, 256 : 256 + ROWS * COLS],
        grad_expanded[...],
        (((1,), (1,)), ((), ())),
        preferred_element_type=f32,
    )
    tap_rows[...] = jnp.zeros((16, 128), f32)
    for k in range(9):
        tap_rows[k : k + 1, :] = jnp.sum(kernel_sums[k].T, axis=0, keepdims=True)
    scaled = proj_grad[...] * coef[0:1, :]
    low = lanes_of((CH, 128)) < 64
    first = join_low(exp_grad, scaled, low).astype(bf16)
    second = join_high(exp_grad, scaled, low).astype(bf16)
    first_taps = tap_rows[...]
    second_taps = pltpu.roll(first_taps, 64, 1)
    for yh in range(2):
        for z in range(8):
            rows = slice((z * 2 + yh) * 16, (z * 2 + yh) * 16 + 16)
            pieces[yh, 0, z] = first[rows]
            pieces[yh, 1, z] = second[rows]
        pieces[yh, 0, 8] = first_taps.astype(bf16)
        pieces[yh, 1, 8] = second_taps.astype(bf16)


def backward(pos, coef, small, normed, act1, slope1, part_p, part_q, proj_grad):
    def along(width):
        return pl.BlockSpec((128, width * COLS), lambda g, pos: (g, 0))

    return pl.pallas_call(
        backward_kernel,
        grid_spec=pltpu.PrefetchScalarGridSpec(
            num_scalar_prefetch=1,
            grid=(BLOCKS,),
            in_specs=[
                pl.BlockSpec((8, 128), lambda g, pos: (0, g)),
                pl.BlockSpec((2, 1, 80, 128), lambda g, pos: (g, pos[0], 0, 0)),
                pl.BlockSpec((CH, EXT * COLS), lambda g, pos: (0, 0)),
                along(EXT),
                along(ROWS),
                along(ROWS + 2),
                along(ROWS + 2),
                pl.BlockSpec((CH, 128), lambda g, pos: (0, g)),
            ],
            out_specs=[
                along(ROWS),
                pl.BlockSpec((2, 2, 9, 16, 128), lambda g, pos: (0, g, 0, 0, 0)),
            ],
            scratch_shapes=[
                pltpu.VMEM((9, 128, 128), f32),
                pltpu.VMEM((128, 128), f32),
                pltpu.VMEM((128, 128), f32),
                pltpu.VMEM((9, 128, 128), f32),
                pltpu.VMEM((16, 128), f32),
            ],
        ),
        out_shape=[
            jax.ShapeDtypeStruct((HALF, ROWS * COLS), bf16),
            jax.ShapeDtypeStruct((2, 8, 9, 16, 128), bf16),
        ],
        compiler_params=params(),
        cost_estimate=cost(8 * 10**9, 30 * 10**6),
        name="backward",
    )(pos, coef, small, normed, act1, slope1, part_p, part_q, proj_grad)


def part_kernel(pos, coef, w_proj, w_exp, act2, grad_expanded, out):
    gated = (w_proj[...].astype(f32) * coef[0:1, :]).astype(bf16)
    for row in range(7):
        cells = slice(row * 128, row * 128 + 128)
        out[0, row] = jnp.dot(gated, act2[:, cells], preferred_element_type=f32).astype(bf16)
        out[1, row] = jnp.dot(
            w_exp[...], grad_expanded[:, cells], preferred_element_type=f32
        ).astype(bf16)


def other_part(pos, coef, w_proj, w_exp, act2, grad_expanded):
    weight = pl.BlockSpec((CH, HALF), lambda g, pos: (0, 0))
    other = pl.BlockSpec((HALF, 7 * COLS), lambda g, pos: (0, 1 - pos[0]))
    return pl.pallas_call(
        part_kernel,
        grid_spec=pltpu.PrefetchScalarGridSpec(
            num_scalar_prefetch=1,
            grid=(1,),
            in_specs=[
                pl.BlockSpec((8, HALF), lambda g, pos: (0, 0)),
                weight,
                weight,
                other,
                other,
            ],
            out_specs=pl.BlockSpec((2, 7, CH, COLS), lambda g, pos: (0, 0, 0, 0)),
        ),
        out_shape=jax.ShapeDtypeStruct((2, 7, CH, COLS), bf16),
        compiler_params=params(),
        cost_estimate=cost(2 * 10**9, 4 * 10**6),
        name="other_part",
    )(pos, coef, w_proj, w_exp, act2, grad_expanded)


def finish_kernel(pos, coef, w_proj, w_exp, act2, grad_expanded, arrived, x, c, block_out, input_grad):
    gated = (w_proj[...].astype(f32) * coef[0:1, :]).astype(bf16)
    for row in range(7):
        cells = slice(row * 128, row * 128 + 128)
        projected = jnp.dot(gated, act2[:, cells], preferred_element_type=f32)
        projected = projected + arrived[0, row].astype(f32)
        values = x[row, 0].astype(f32)
        block_out[row, 0] = (values + projected).astype(bf16)
        grad = jnp.dot(w_exp[...], grad_expanded[:, cells], preferred_element_type=f32)
        grad = grad + arrived[1, row].astype(f32)
        center = values - jnp.mean(values, axis=0, keepdims=True)
        inv_std = lax.rsqrt(jnp.mean(center * center, axis=0, keepdims=True) + 1e-05)
        normal = center * inv_std
        mean_grad = jnp.mean(grad, axis=0, keepdims=True)
        mean_inner = jnp.mean(grad * normal, axis=0, keepdims=True)
        input_grad[row, 0] = (
            c[row, 0].astype(f32) + inv_std * (grad - mean_grad - normal * mean_inner)
        ).astype(bf16)


def finish(pos, coef, w_proj, w_exp, act2, grad_expanded, arrived, x, c):
    weight = pl.BlockSpec((CH, HALF), lambda g, pos: (0, 0))
    own = pl.BlockSpec((HALF, 7 * COLS), lambda g, pos: (0, pos[0]))
    rows = pl.BlockSpec((7, 1, CH, COLS), lambda g, pos: (0, 0, 0, 0))
    return pl.pallas_call(
        finish_kernel,
        grid_spec=pltpu.PrefetchScalarGridSpec(
            num_scalar_prefetch=1,
            grid=(1,),
            in_specs=[
                pl.BlockSpec((8, HALF), lambda g, pos: (0, 0)),
                weight,
                weight,
                own,
                own,
                pl.BlockSpec((2, 7, CH, COLS), lambda g, pos: (0, 0, 0, 0)),
                rows,
                rows,
            ],
            out_specs=[rows, rows],
        ),
        out_shape=[jax.ShapeDtypeStruct((7, 1, CH, COLS), bf16)] * 2,
        compiler_params=params(),
        cost_estimate=cost(2 * 10**9, 6 * 10**6),
        name="finish",
    )(pos, coef, w_proj, w_exp, act2, grad_expanded, arrived, x, c)


def body(inputs, cotangent, w_expand, w_project, dw_kernel, se_down, se_up):
    place = lax.axis_index("tensor")
    core = lax.rem(place, 2)
    chip = lax.div(place, 2)
    pos = jnp.stack([core, (chip > 0), (chip < 7), chip]).astype(jnp.int32)
    swap = [(i, i ^ 1) for i in range(16)]
    with jax.named_scope("weights"):
        piece = jnp.concatenate([w_expand, w_project], axis=1)
        lines = exchange(to_all(piece, 8), "dp", DEPTH)
        weights = exchange(to_all(lines, 16), BOTH, PLANE).reshape(2, 8, 8, 16, 128)
    with jax.named_scope("small"):
        tap_rows = jnp.pad(dw_kernel.T, ((0, 7), (0, 64)))
        small = jnp.concatenate([jnp.concatenate([se_down, se_up], axis=1), tap_rows], axis=0)
        small = exchange(to_all(small, 16), "tensor")
        small_pairs = small.reshape(8, 2, 80, 128)
    with jax.named_scope("rows"):
        other_x = lax.ppermute(inputs, "tensor", swap)
        other_c = lax.ppermute(cotangent, "tensor", swap)
        last = jnp.where(
            core == 1,
            jnp.stack([inputs[5:7, 0], cotangent[5:7, 0]]),
            jnp.stack([other_x[5:7, 0], other_c[5:7, 0]]),
        )
        first = jnp.where(
            core == 0,
            jnp.stack([inputs[0:2, 0], cotangent[0:2, 0]]),
            jnp.stack([other_x[0:2, 0], other_c[0:2, 0]]),
        )
        top = lax.ppermute(last, "tensor", [(i, i + 2) for i in range(14)])
        bottom = lax.ppermute(first, "tensor", [(i + 2, i) for i in range(14)])
    normed, cot = norm_rows(pos, inputs, other_x, cotangent, other_c, top, bottom)
    act1, slope1, act2, part_p, part_q, proj_grad, w_exp, w_proj, sums = forward(
        pos, weights, small_pairs, normed, cot
    )
    with jax.named_scope("sums"):
        all_sums = exchange(to_all(sums, 16), "tensor")
    coef, vectors = excite(pos, all_sums, small)
    with jax.named_scope("vectors"):
        all_vectors = exchange(to_all(vectors, 16), "dp")
        swish, grad_squeeze = all_vectors[:, 0, :64], all_vectors[:, 0, 64:]
        pooled, grad_excite = all_vectors[:, 1, :64], all_vectors[:, 1, 64:]
        highest = lax.Precision.HIGHEST
        up_grad = jnp.einsum("is,ie->se", swish, grad_excite, precision=highest)
        down_grad = jnp.einsum("is,ie->se", grad_squeeze, pooled, precision=highest)
    grad_expanded, pieces = backward(
        pos, coef, small_pairs, normed, act1, slope1, part_p, part_q, proj_grad
    )
    with jax.named_scope("gradients"):
        pieces = exchange(pieces.reshape(16, 9, 16, 128), BOTH, PLANE)
        partial = jnp.sum(pieces.astype(f32), axis=0).astype(bf16)
        lines = jnp.stack([partial[:8], to_all(partial[8], 8)], axis=1)
        lines = exchange(lines, "dp", DEPTH)
        total = jnp.sum(lines.astype(f32), axis=0)
    with jax.named_scope("finish"):
        partial_out = other_part(pos, coef, w_proj, w_exp, act2, grad_expanded)
        arrived = lax.ppermute(partial_out, "tensor", swap)
        block_out, input_grad = finish(
            pos, coef, w_proj, w_exp, act2, grad_expanded, arrived, inputs, cotangent
        )
    return (
        block_out,
        input_grad,
        total[0, :, :64],
        total[0, :, 64:],
        total[1, :9, :64].T,
        down_grad,
        up_grad,
    )


def solution(mesh):
    placed = (
        P("tensor", "dp", None, None),
        P("tensor", "dp", None, None),
        P("dp", "tensor"),
        P("dp", "tensor"),
        P("tensor", None),
        P(None, "tensor"),
        P(None, "tensor"),
    )
    return jax.shard_map(
        body,
        mesh=mesh,
        in_specs=placed,
        out_specs=(
            P("tensor", "dp", None, None),
            P("tensor", "dp", None, None),
            P("dp", "tensor"),
            P("dp", "tensor"),
            P("tensor", None),
            P(None, "tensor"),
            P(None, "tensor"),
        ),
        check_vma=False,
    )
```

```python
import jax
import jax.numpy as jnp
from jax import lax
from jax.experimental import pallas as pl
from jax.experimental.pallas import tpu as pltpu
from jax.sharding import PartitionSpec as P

bf16 = jnp.bfloat16
f32 = jnp.float32

gelu_scale = 0.7978845608
gelu_cubic = 0.044715

CH = 256
HALF = 512
SQ = 64
COLS = 128
ROWS = 14
EXT = ROWS + 4
CELLS = 112 * 128
BLOCKS = 4
GROUP = 16
BOTH = ("dp", "tensor")
VMEM = 16 * 1024 * 1024
SMALL = 10**5


def groups(count, steps):
    seen, found = set(), []
    for first in range(count):
        if first in seen:
            continue
        members = [first]
        for step in steps:
            members = members + [member ^ step for member in members]
        members = sorted(members)
        seen.update(members)
        found.append(members)
    return found


def exchange(pieces, axes, steps=None):
    members = None
    if steps is not None:
        members = groups(256 if axes == BOTH else 16, steps)
    return lax.all_to_all(pieces, axes, 0, 0, tiled=True, axis_index_groups=members)


def to_all(piece, count):
    return jnp.broadcast_to(piece[None], (count,) + piece.shape)


PLANE = (2, 4, 8, 16)
DEPTH = (2, 4, 8)


def gelu_pair(values):
    square = values * values
    inner = values * (gelu_scale + (gelu_scale * gelu_cubic) * square)
    part = 0.5 + 0.5 * jnp.tanh(inner)
    act = values * part
    slope = part + act * (1.0 - part) * (
        2.0 * gelu_scale + (6.0 * gelu_scale * gelu_cubic) * square
    )
    return act, slope


def params(**more):
    return pltpu.CompilerParams(vmem_limit_bytes=VMEM, **more)


def cost(flops, size):
    return pl.CostEstimate(flops=flops, bytes_accessed=size, transcendentals=0)


def join_low(first, second, low):
    return jnp.where(low, first, pltpu.roll(second, 64, 1))


def join_high(first, second, low):
    return jnp.where(low, pltpu.roll(first, 64, 1), second)


def full(*shape):
    return pl.BlockSpec(shape, lambda *unused: (0,) * len(shape))


def in_vmem(count):
    return [pl.BlockSpec(memory_space=pltpu.VMEM)] * count


def in_hbm(count):
    return [pl.BlockSpec(memory_space=pltpu.HBM)] * count


def held(shape, kind):
    return pltpu.VMEM(shape, kind)


def kept(*arrays):
    return [pltpu.with_memory_space_constraint(array, pltpu.VMEM) for array in arrays]


def far_memory(*arrays):
    return [pltpu.with_memory_space_constraint(array, pltpu.HBM) for array in arrays]


def tensor_place():
    place = lax.axis_index("tensor")
    return lax.rem(place, 2), lax.div(place, 2)


def image_place():
    image = lax.axis_index("dp")
    return lax.div(image, 2), lax.rem(image, 2)


def lanes_of(shape):
    return lax.broadcasted_iota(jnp.int32, shape, 1)


def down_rows(row):
    return jnp.broadcast_to(row, (128, 128)).T


def start_kernel(
    x, c, w_expand, w_project, dw_rows, se_down, se_up,
    packed, edge,
    tall, wide, expand_in, project_in, dw_in, down_in, up_in, sems,
):
    core, _ = tensor_place()
    z, yh = image_place()
    pairs = (
        (w_expand, expand_in),
        (w_project, project_in),
        (dw_rows, dw_in),
        (se_down, down_in),
        (se_up, up_in),
        (x.at[pl.ds(5 * core, 2)], edge.at[0]),
        (c.at[pl.ds(5 * core, 2)], edge.at[1]),
    )
    copies = [pltpu.make_async_copy(a, b, sems.at[i]) for i, (a, b) in enumerate(pairs)]
    for copy in copies:
        copy.start()
    wide[0:16, :] = jnp.zeros((16, 128), f32)
    for copy in copies[:5]:
        copy.wait()
    wide[0:9, 0:64] = dw_in[...].astype(f32)
    tall[0:64, 0:64] = down_in[...].astype(f32)
    tall[0:64, 64:128] = up_in[...].astype(f32)
    wide[16:32, 0:64] = expand_in[...].astype(f32)
    wide[16:32, 64:128] = project_in[...].astype(f32)
    squeeze_rows = tall[pl.ds(yh * 32 + z * 4, 4), :]
    tap_row = wide[pl.ds(yh * 8 + z, 1), :]
    tall[16:32, :] = jnp.zeros((16, 128), f32)
    tall[16:20, :] = squeeze_rows
    tall[20:21, :] = tap_row
    piece = jnp.concatenate([wide[16:32, :], tall[16:32, :]], axis=0).astype(bf16)
    for other in range(8):
        packed[other] = piece
    for copy in copies[5:]:
        copy.wait()


def start(x, c, w_expand, w_project, dw_rows, se_down, se_up):
    return pl.pallas_call(
        start_kernel,
        in_specs=in_hbm(7),
        out_specs=in_vmem(2),
        out_shape=[
            jax.ShapeDtypeStruct((8, 32, 128), bf16),
            held((2, 2, 1, CH, COLS), bf16),
        ],
        scratch_shapes=[
            pltpu.VMEM((64, 128), f32),
            pltpu.VMEM((32, 128), f32),
            pltpu.VMEM((16, 64), bf16),
            pltpu.VMEM((16, 64), bf16),
            pltpu.VMEM((9, 64), bf16),
            pltpu.VMEM((64, 64), bf16),
            pltpu.VMEM((64, 64), bf16),
            pltpu.SemaphoreType.DMA((7,)),
        ],
        compiler_params=params(),
        cost_estimate=cost(SMALL, SMALL),
        name="start",
    )(*far_memory(x, c, w_expand, w_project, dw_rows, se_down, se_up))


def spread_kernel(lines, first, second, out, squeeze_rows, tap_rows):
    tap_rows[...] = jnp.zeros((16, 128), f32)
    for z in range(8):
        small = lines[z, 16:32, :].astype(f32)
        squeeze_rows[z * 4 : z * 4 + 4, :] = small[0:4]
        tap_rows[z : z + 1, :] = small[4:5]
    squeeze_piece = squeeze_rows[...].astype(bf16)
    tap_piece = tap_rows[...].astype(bf16)
    for other in range(16):
        for z in range(8):
            out[other, z] = lines[z, 0:16, :]
        out[other, 8] = squeeze_piece[0:16]
        out[other, 9] = squeeze_piece[16:32]
        out[other, 10] = tap_piece


def spread(lines, first, second):
    return pl.pallas_call(
        spread_kernel,
        in_specs=in_vmem(3),
        out_specs=in_vmem(1)[0],
        out_shape=jax.ShapeDtypeStruct((16, 11, 16, 128), bf16),
        scratch_shapes=[pltpu.VMEM((32, 128), f32), pltpu.VMEM((16, 128), f32)],
        compiler_params=params(),
        cost_estimate=cost(SMALL, SMALL),
        name="spread",
    )(lines, first, second)


def normal_of(x):
    values = x.astype(f32)
    center = values - jnp.mean(values, axis=0, keepdims=True)
    inv_std = lax.rsqrt(jnp.mean(center * center, axis=0, keepdims=True) + 1e-05)
    return (center * inv_std).astype(bf16)


def lane_block(row):
    return pl.ds(pl.multiple_of(row * 128, 128), 128)


def main_norm_kernel(own_x, other_x, own_c, other_c, normed, cot, done):
    done[...] = jnp.zeros((8, 128), f32)
    core, _ = tensor_place()
    for x, c, first in ((own_x, own_c, 7 * core), (other_x, other_c, 7 - 7 * core)):
        for row in range(7):
            normed[:, lane_block(first + row)] = normal_of(x[row, 0])
            cot[:, lane_block(first + row)] = c[row, 0]


def main_norm(own_x, other_x, own_c, other_c):
    return pl.pallas_call(
        main_norm_kernel,
        in_specs=in_vmem(4),
        out_specs=in_vmem(3),
        out_shape=[held((CH, ROWS * COLS), bf16)] * 2 + [jax.ShapeDtypeStruct((8, 128), f32)],
        compiler_params=params(),
        cost_estimate=cost(SMALL, SMALL),
        name="main_norm",
    )(own_x, other_x, own_c, other_c)


def edge_norm_kernel(near, far, normed, cot, done):
    done[...] = jnp.zeros((8, 128), f32)
    core, _ = tensor_place()
    for edge, first in ((near, 2 * core), (far, 2 - 2 * core)):
        for row in range(2):
            normed[:, lane_block(first + row)] = normal_of(edge[0, row, 0])
            cot[:, lane_block(first + row)] = edge[1, row, 0]


def edge_norm(near, far):
    return pl.pallas_call(
        edge_norm_kernel,
        in_specs=in_vmem(2),
        out_specs=in_vmem(3),
        out_shape=[held((CH, 4 * COLS), bf16)] * 2 + [jax.ShapeDtypeStruct((8, 128), f32)],
        compiler_params=params(),
        cost_estimate=cost(SMALL, SMALL),
        name="edge_norm",
    )(near, far)


def spread_taps(sources, taps, place, masked):
    low = lanes_of((16, 128)) < 64
    early = join_low(sources[0][0].astype(f32), sources[0][1].astype(f32), low)
    late = join_low(sources[1][0].astype(f32), sources[1][1].astype(f32), low)
    lane = lanes_of((128, 128))
    for tap in range(9):
        spread = down_rows(early[tap : tap + 1, :] if tap < 8 else late[0:1, :])
        if masked and tap % 3 == 0:
            spread = jnp.where(lane == 0, 0.0, spread)
        if masked and tap % 3 == 2:
            spread = jnp.where(lane == 127, 0.0, spread)
        taps[tap, place : place + 128, :] = spread


def forward_kernel(
    weights, normed, cot, normed_edge, cot_edge,
    normed_out, act1, slope1, act2, part_p, part_q, proj_grad, w_exp, w_proj, squeeze_rows, sums,
    expanded, grad_hidden, taps, pool, gate,
):
    _, chip = tensor_place()
    normed_out[...] = normed[...]
    low = lanes_of((16, 128)) < 64
    for block in range(BLOCKS):
        cells = slice(block * 128, block * 128 + 128)
        for z in range(8):
            for yh in range(2):
                first = weights[yh, 2 * block, z].astype(f32)
                second = weights[yh, 2 * block + 1, z].astype(f32)
                rows = slice((z * 2 + yh) * 16, (z * 2 + yh) * 16 + 16)
                w_exp[rows, cells] = join_low(first, second, low).astype(bf16)
                w_proj[rows, cells] = join_high(first, second, low).astype(bf16)
        spread_taps(
            [[weights[yh, 2 * block + j, 10] for j in range(2)] for yh in range(2)],
            taps,
            block * 128,
            True,
        )
    squeeze_rows[...] = weights[:, :, 8:10]
    w_exp_t = w_exp[...].astype(f32).T.astype(bf16)
    w_proj_t = w_proj[...].astype(f32).T.astype(bf16)

    def multiply(weight, source, target, place):
        target[:, place * 128 : place * 128 + source.shape[1]] = jnp.dot(
            weight, source, preferred_element_type=f32
        ).astype(bf16)

    multiply(w_exp_t, normed_edge[:, 0:256], expanded, 0)
    multiply(w_exp_t, normed_edge[:, 256:512], expanded, ROWS + 2)
    multiply(w_proj_t, cot_edge[:, 128:256], grad_hidden, 0)
    multiply(w_proj_t, cot_edge[:, 256:384], grad_hidden, ROWS + 1)
    for part in range(ROWS // 2):
        cells = slice(part * 256, part * 256 + 256)
        multiply(w_exp_t, normed[:, cells], expanded, 2 + 2 * part)
        multiply(w_proj_t, cot[:, cells], grad_hidden, 1 + 2 * part)
    first_chip = jnp.where(chip > 0, 1.0, 0.0)
    last_chip = jnp.where(chip < 7, 1.0, 0.0)

    def one_group(index, carry):
        rows = pl.ds(pl.multiple_of(index * GROUP, GROUP), GROUP)
        tap = [taps[k, rows, :] for k in range(9)]
        running = {}
        pool_sum = jnp.zeros((GROUP, COLS), f32)
        gate_sum = jnp.zeros((GROUP, COLS), f32)
        for h in range(EXT):
            value = expanded[rows, h * 128 : h * 128 + 128].astype(f32)
            act, slope = gelu_pair(value)
            act1[rows, h * 128 : h * 128 + 128] = act.astype(bf16)
            if 2 <= h < ROWS + 2:
                slope1[rows, (h - 2) * 128 : (h - 1) * 128] = slope.astype(bf16)
            left = pltpu.roll(act, 1, 1)
            right = pltpu.roll(act, 127, 1)
            for i in range(3):
                m = h + 1 - i
                if not 1 <= m <= ROWS + 2:
                    continue
                term = tap[3 * i] * left + tap[3 * i + 1] * act + tap[3 * i + 2] * right
                running[m] = running[m] + term if m in running else term
            m = h - 1
            if not 1 <= m <= ROWS + 2:
                continue
            act, slope = gelu_pair(running.pop(m))
            grad = grad_hidden[rows, (m - 1) * 128 : m * 128].astype(f32)
            if m == 1:
                slope = slope * first_chip
            if m == ROWS + 2:
                slope = slope * last_chip
            part_q[rows, (m - 1) * 128 : m * 128] = slope.astype(bf16)
            part_p[rows, (m - 1) * 128 : m * 128] = (slope * grad).astype(bf16)
            if 2 <= m < ROWS + 2:
                act2[rows, (m - 2) * 128 : (m - 1) * 128] = act.astype(bf16)
                pool_sum = pool_sum + act
                gate_sum = gate_sum + act * grad
        pool[rows, :] = pool_sum
        gate[rows, :] = gate_sum
        return carry

    lax.fori_loop(0, HALF // GROUP, one_group, 0)
    for block in range(BLOCKS):
        cells = slice(block * 128, block * 128 + 128)
        pool_row = jnp.sum(pool[cells, :].T, axis=0, keepdims=True)
        gate_row = jnp.sum(gate[cells, :].T, axis=0, keepdims=True)
        for other in range(16):
            sums[other, block : block + 1, :] = pool_row
            sums[other, BLOCKS + block : BLOCKS + block + 1, :] = gate_row
    proj_grad[...] = lax.dot_general(
        cot[...], act2[...], (((1,), (1,)), ((), ())), preferred_element_type=f32
    )


def forward(weights, normed, cot, normed_edge, cot_edge):
    return pl.pallas_call(
        forward_kernel,
        in_specs=in_vmem(5),
        out_specs=in_vmem(11),
        scratch_shapes=[
            pltpu.VMEM((HALF, EXT * COLS), bf16),
            pltpu.VMEM((HALF, (ROWS + 2) * COLS), bf16),
            pltpu.VMEM((9, HALF, 128), f32),
            pltpu.VMEM((HALF, 128), f32),
            pltpu.VMEM((HALF, 128), f32),
        ],
        out_shape=[
            held((CH, ROWS * COLS), bf16),
            held((HALF, EXT * COLS), bf16),
            held((HALF, ROWS * COLS), bf16),
            held((HALF, ROWS * COLS), bf16),
            held((HALF, (ROWS + 2) * COLS), bf16),
            held((HALF, (ROWS + 2) * COLS), bf16),
            held((CH, HALF), f32),
            held((CH, HALF), bf16),
            held((CH, HALF), bf16),
            held((2, 8, 2, 16, 128), bf16),
            jax.ShapeDtypeStruct((16, 8, 128), f32),
        ],
        compiler_params=params(),
        cost_estimate=cost(10**9, 50 * 10**6),
        name="forward",
    )(weights, *kept(normed, cot, normed_edge, cot_edge))


def excite_kernel(sums, own_rows, other_rows, coef):
    low = lanes_of((SQ, 128)) < 64
    totals = []
    for half in range(2):
        total = sums[half]
        for other in range(1, 8):
            total = total + sums[2 * other + half]
        totals.append(total)
    core, _ = tensor_place()
    is_first = core == 0
    ordered = (
        jnp.where(is_first, totals[0], totals[1]),
        jnp.where(is_first, totals[1], totals[0]),
    )
    pooled, grad_gate, down, up = [], [], [], []
    for total, rows in zip(ordered, (own_rows, other_rows)):
        for block in range(BLOCKS):
            pooled.append(total[block : block + 1] * (1.0 / CELLS))
            grad_gate.append(total[BLOCKS + block : BLOCKS + block + 1])
            halves = [
                jnp.concatenate(
                    [rows[yh, 2 * block + j, part].astype(f32) for yh in range(2) for part in range(2)],
                    axis=0,
                )
                for j in range(2)
            ]
            down.append(join_low(halves[0], halves[1], low))
            up.append(join_high(halves[0], halves[1], low))
    count = 2 * BLOCKS
    squeeze = sum(jnp.sum(down[b] * pooled[b], axis=1, keepdims=True) for b in range(count))
    sig = 1.0 / (1.0 + jnp.exp(-squeeze))
    swish = squeeze * sig
    gating, grad_excite = [], []
    for b in range(count):
        logit = jnp.sum(up[b] * swish, axis=0, keepdims=True)
        gating.append(1.0 / (1.0 + jnp.exp(-logit)))
        grad_excite.append(grad_gate[b] * gating[b] * (1.0 - gating[b]))
    grad_swish = sum(jnp.sum(up[b] * grad_excite[b], axis=1, keepdims=True) for b in range(count))
    grad_squeeze = grad_swish * sig * (1.0 + squeeze * (1.0 - sig))
    side = jnp.concatenate([swish, grad_squeeze], axis=0)
    side_row = jnp.broadcast_to(side, (128, 128)).T[0:1, :]
    for b in range(BLOCKS):
        cells = slice(b * 128, b * 128 + 128)
        grad_pooled = jnp.sum(down[b] * grad_squeeze, axis=0, keepdims=True)
        coef[0:1, cells] = gating[b]
        coef[1:2, cells] = grad_pooled * (1.0 / CELLS)
        coef[2:3, cells] = pooled[b]
        coef[3:4, cells] = grad_excite[b]
        coef[4:5, cells] = side_row
    coef[5:8, :] = jnp.zeros((3, HALF), f32)


def excite(sums, own_rows, other_rows):
    return pl.pallas_call(
        excite_kernel,
        in_specs=in_vmem(3),
        out_specs=in_vmem(1)[0],
        out_shape=held((8, HALF), f32),
        compiler_params=params(),
        cost_estimate=cost(SMALL, 4 * 10**6),
        name="excite",
    )(sums, *kept(own_rows), other_rows)


def backward_kernel(
    coef, weights, normed, act1, slope1, part_p, part_q, proj_grad, w_proj, w_exp, act2,
    grad_out, pieces, other_out,
    grad_expanded, copied,
    taps, gates, pools, kernel_sums, tap_rows,
):
    for block in range(BLOCKS):
        cells = slice(block * 128, block * 128 + 128)
        spread_taps(
            [[weights[yh, 2 * block + j, 10] for j in range(2)] for yh in range(2)],
            taps,
            block * 128,
            False,
        )
        gates[cells, :] = down_rows(coef[0:1, cells])
        pools[cells, :] = down_rows(coef[1:2, cells])
    lane = lanes_of((GROUP, COLS))

    def one_group(index, carry):
        rows = pl.ds(pl.multiple_of(index * GROUP, GROUP), GROUP)
        tap = [taps[k, rows, :] for k in range(9)]
        gating = gates[rows, :]
        pooled = pools[rows, :]
        running = {}
        sums = [None] * 9
        for m in range(1, ROWS + 3):
            cells = slice((m - 1) * 128, m * 128)
            grad = part_p[rows, cells].astype(f32) * gating + part_q[rows, cells].astype(f32) * pooled
            turned = (
                jnp.where(lane == 127, 0.0, pltpu.roll(grad, 127, 1)),
                grad,
                jnp.where(lane == 0, 0.0, pltpu.roll(grad, 1, 1)),
            )
            for i in range(3):
                h = m + i - 1
                if 2 <= h < ROWS + 2:
                    term = tap[3 * i] * turned[0] + tap[3 * i + 1] * turned[1] + tap[3 * i + 2] * turned[2]
                    running[h] = running[h] + term if h in running else term
                if 2 <= m < ROWS + 2:
                    act = act1[rows, h * 128 : h * 128 + 128].astype(f32)
                    for j in range(3):
                        term = turned[j] * act
                        k = 3 * i + j
                        sums[k] = term if sums[k] is None else sums[k] + term
            h = m - 1
            if 2 <= h < ROWS + 2:
                out = slice((h - 2) * 128, (h - 1) * 128)
                grad_expanded[rows, out] = (running.pop(h) * slope1[rows, out].astype(f32)).astype(bf16)
        for k in range(9):
            kernel_sums[k, rows, :] = sums[k]
        return carry

    lax.fori_loop(0, HALF // GROUP, one_group, 0)
    copy_out = pltpu.make_async_copy(grad_expanded, grad_out, copied)
    copy_out.start()
    core, _ = tensor_place()
    cells = pl.ds(pl.multiple_of((1 - core) * (7 * COLS), 7 * COLS), 7 * COLS)
    gated = (w_proj[...].astype(f32) * coef[0:1, :]).astype(bf16)
    projected = jnp.dot(gated, act2[:, cells], preferred_element_type=f32).astype(bf16)
    grad = jnp.dot(w_exp[...], grad_expanded[:, cells], preferred_element_type=f32).astype(bf16)
    for row in range(7):
        other_out[0, row] = projected[:, row * 128 : row * 128 + 128]
        other_out[1, row] = grad[:, row * 128 : row * 128 + 128]
    exp_grad = lax.dot_general(
        normed[...], grad_expanded[...], (((1,), (1,)), ((), ())), preferred_element_type=f32
    )
    low = lanes_of((CH, 128)) < 64
    tap_low = lanes_of((1, 128)) < 64
    tap_rows[...] = jnp.zeros((16, 128), f32)
    for block in range(BLOCKS):
        cells = slice(block * 128, block * 128 + 128)
        scaled = proj_grad[:, cells] * coef[0:1, cells]
        first = join_low(exp_grad[:, cells], scaled, low).astype(bf16)
        second = join_high(exp_grad[:, cells], scaled, low).astype(bf16)
        for k in range(9):
            tap_rows[k : k + 1, :] = jnp.sum(kernel_sums[k, cells, :].T, axis=0, keepdims=True)
        tap_rows[9:10, :] = join_low(coef[2:3, cells], coef[3:4, cells], tap_low)
        tap_rows[10:11, :] = coef[4:5, cells]
        first_taps = tap_rows[...].astype(bf16)
        tap_rows[0:9, :] = pltpu.roll(tap_rows[...], 64, 1)[0:9]
        tap_rows[9:10, :] = join_high(coef[2:3, cells], coef[3:4, cells], tap_low)
        second_taps = tap_rows[...].astype(bf16)
        for yh in range(2):
            for z in range(8):
                rows = slice((z * 2 + yh) * 16, (z * 2 + yh) * 16 + 16)
                pieces[yh, 2 * block, z] = first[rows]
                pieces[yh, 2 * block + 1, z] = second[rows]
            pieces[yh, 2 * block, 8] = first_taps
            pieces[yh, 2 * block + 1, 8] = second_taps
    copy_out.wait()


def backward(coef, weights, normed, act1, slope1, part_p, part_q, proj_grad, w_proj, w_exp, act2):
    return pl.pallas_call(
        backward_kernel,
        in_specs=in_vmem(11),
        out_specs=in_hbm(1) + in_vmem(2),
        scratch_shapes=[
            pltpu.VMEM((HALF, ROWS * COLS), bf16),
            pltpu.SemaphoreType.DMA,
            pltpu.VMEM((9, HALF, 128), f32),
            pltpu.VMEM((HALF, 128), f32),
            pltpu.VMEM((HALF, 128), f32),
            pltpu.VMEM((9, HALF, 128), f32),
            pltpu.VMEM((16, 128), f32),
        ],
        out_shape=[
            pltpu.HBM((HALF, ROWS * COLS), bf16),
            pltpu.HBM((2, 8, 9, 16, 128), bf16),
            jax.ShapeDtypeStruct((2, 7, CH, COLS), bf16),
        ],
        compiler_params=params(),
        cost_estimate=cost(10**9, 45 * 10**6),
        name="backward",
    )(
        *kept(
            coef, weights, normed, act1, slope1, part_p, part_q, proj_grad, w_proj, w_exp, act2
        )
    )


def finish_kernel(coef, w_proj, w_exp, act2, grad_expanded, arrived, x, c, block_out, input_grad, done):
    core, _ = tensor_place()
    cells = pl.ds(pl.multiple_of(core * (7 * COLS), 7 * COLS), 7 * COLS)
    gated = (w_proj[...].astype(f32) * coef[0:1, :]).astype(bf16)
    done[...] = jnp.zeros((8, 128), f32)
    all_projected = jnp.dot(gated, act2[:, cells], preferred_element_type=f32)
    all_grad = jnp.dot(w_exp[...], grad_expanded[:, cells], preferred_element_type=f32)
    for row in range(7):
        projected = all_projected[:, row * 128 : row * 128 + 128] + arrived[0, row].astype(f32)
        values = x[row, 0].astype(f32)
        block_out[row, 0] = (values + projected).astype(bf16)
        grad = all_grad[:, row * 128 : row * 128 + 128] + arrived[1, row].astype(f32)
        center = values - jnp.mean(values, axis=0, keepdims=True)
        inv_std = lax.rsqrt(jnp.mean(center * center, axis=0, keepdims=True) + 1e-05)
        normal = center * inv_std
        mean_grad = jnp.mean(grad, axis=0, keepdims=True)
        mean_inner = jnp.mean(grad * normal, axis=0, keepdims=True)
        input_grad[row, 0] = (
            c[row, 0].astype(f32) + inv_std * (grad - mean_grad - normal * mean_inner)
        ).astype(bf16)


def finish(coef, w_proj, w_exp, act2, grad_expanded, arrived, x, c):
    return pl.pallas_call(
        finish_kernel,
        in_specs=in_vmem(8),
        out_specs=in_vmem(3),
        out_shape=[
            jax.ShapeDtypeStruct((7, 1, CH, COLS), bf16),
            jax.ShapeDtypeStruct((7, 1, CH, COLS), bf16),
            jax.ShapeDtypeStruct((8, 128), f32),
        ],
        compiler_params=params(),
        cost_estimate=cost(SMALL, SMALL),
        name="finish",
    )(*kept(coef, w_proj, w_exp, act2), grad_expanded, arrived, x, c)


def middle_kernel(pieces, after, out):
    for slot in range(9):
        total = pieces[0, slot].astype(f32)
        for other in range(1, 16):
            total = total + pieces[other, slot].astype(f32)
        total = total.astype(bf16)
        if slot < 8:
            out[slot, 0] = total
        else:
            for z in range(8):
                out[z, 1] = total
    low = lanes_of((SQ, 128)) < 64
    outer = jnp.zeros((SQ, 128), f32)
    for yh in range(2):
        vectors = pieces[yh * 8, 8].astype(f32)
        column = down_rows(vectors[10:11, :])
        outer = outer + jnp.where(low, column[64:128], column[0:64]) * vectors[9:10, :]
    outer = outer.astype(bf16)
    for z in range(8):
        for part in range(4):
            out[z, 2 + part] = outer[part * 16 : part * 16 + 16]


def middle(pieces, after):
    return pl.pallas_call(
        middle_kernel,
        in_specs=in_vmem(2),
        out_specs=in_vmem(1)[0],
        out_shape=jax.ShapeDtypeStruct((8, 6, 16, 128), bf16),
        compiler_params=params(),
        cost_estimate=cost(10**6, 4 * 10**6),
        name="middle",
    )(pieces, after)


def tail_kernel(lines, exp_grad, proj_grad, kernel_grad, down_grad, up_grad):
    def total_of(slot):
        total = lines[0, slot].astype(f32)
        for z in range(1, 8):
            total = total + lines[z, slot].astype(f32)
        return total

    first = total_of(0)
    exp_grad[...] = first[:, 0:64]
    proj_grad[...] = pltpu.roll(first, 64, 1)[:, 0:64]
    kernel_grad[...] = total_of(1)[0:9, 0:64]
    for part in range(4):
        both = total_of(2 + part)
        down_grad[part * 16 : part * 16 + 16, :] = both[:, 0:64]
        up_grad[part * 16 : part * 16 + 16, :] = pltpu.roll(both, 64, 1)[:, 0:64]


def tail(lines):
    return pl.pallas_call(
        tail_kernel,
        in_specs=in_vmem(1),
        out_specs=in_vmem(5),
        out_shape=[
            jax.ShapeDtypeStruct((16, 64), f32),
            jax.ShapeDtypeStruct((16, 64), f32),
            jax.ShapeDtypeStruct((9, 64), f32),
            jax.ShapeDtypeStruct((64, 64), f32),
            jax.ShapeDtypeStruct((64, 64), f32),
        ],
        compiler_params=params(),
        cost_estimate=cost(10**6, 2 * 10**6),
        name="tail",
    )(lines)


def body(inputs, cotangent, w_expand, w_project, dw_kernel, se_down, se_up):
    swap = [(i, i ^ 1) for i in range(16)]
    edges = [(i, i + 1) for i in range(1, 14, 2)] + [(i + 1, i) for i in range(1, 14, 2)]
    far_edges = [(i, i + 2) for i in range(1, 14, 2)] + [(i, i - 2) for i in range(2, 16, 2)]
    packed, edge = start(inputs, cotangent, w_expand, w_project, dw_kernel.T, se_down, se_up)
    with jax.named_scope("rows"):
        near = lax.ppermute(edge, "tensor", edges)
        far = lax.ppermute(edge, "tensor", far_edges)
        other_x = lax.ppermute(inputs, "tensor", swap)
        other_c = lax.ppermute(cotangent, "tensor", swap)
        normed, cot, main_done = main_norm(inputs, other_x, cotangent, other_c)
        normed_edge, cot_edge, edge_done = edge_norm(near, far)
    with jax.named_scope("weights"):
        lines = exchange(packed, "dp", DEPTH)
        copies = spread(lines, main_done, edge_done)
        weights = exchange(copies, BOTH, PLANE).reshape(2, 8, 11, 16, 128)
    (
        normed, act1, slope1, act2, part_p, part_q, proj_grad, w_exp, w_proj, own_rows, sums
    ) = forward(weights, normed, cot, normed_edge, cot_edge)
    with jax.named_scope("sums"):
        other_rows = lax.ppermute(own_rows, "tensor", swap)
        all_sums = exchange(sums, "tensor")
    coef = excite(all_sums, own_rows, other_rows)
    grad_expanded, pieces, partial_out = backward(
        coef, weights, normed, act1, slope1, part_p, part_q, proj_grad, w_proj, w_exp, act2
    )
    with jax.named_scope("finish"):
        arrived = lax.ppermute(partial_out, "tensor", swap)
        block_out, input_grad, done = finish(
            coef, w_proj, w_exp, act2, grad_expanded, arrived, inputs, cotangent
        )
    with jax.named_scope("gradients"):
        pieces = exchange(pieces.reshape(16, 9, 16, 128), BOTH, PLANE)
        lines = exchange(middle(pieces, done), "dp", DEPTH)
        exp_grad, proj_grad, kernel_grad, down_grad, up_grad = tail(lines)
    return (block_out, input_grad, exp_grad, proj_grad, kernel_grad.T, down_grad, up_grad)


def solution(mesh):
    placed = (
        P("tensor", "dp", None, None),
        P("tensor", "dp", None, None),
        P("dp", "tensor"),
        P("dp", "tensor"),
        P("tensor", None),
        P(None, "tensor"),
        P(None, "tensor"),
    )
    return jax.shard_map(
        body,
        mesh=mesh,
        in_specs=placed,
        out_specs=(
            P("tensor", "dp", None, None),
            P("tensor", "dp", None, None),
            P("dp", "tensor"),
            P("dp", "tensor"),
            P("tensor", None),
            P(None, "tensor"),
            P(None, "tensor"),
        ),
        check_vma=False,
    )
```

```python
import jax
import jax.numpy as jnp
from jax import lax
from jax.experimental import pallas as pl
from jax.experimental.pallas import tpu as pltpu
from jax.sharding import PartitionSpec as P

bf16 = jnp.bfloat16
f32 = jnp.float32

gelu_scale = 0.7978845608
gelu_cubic = 0.044715

CH = 256
HALF = 512
SQ = 64
COLS = 128
ROWS = 14
EXT = ROWS + 4
CELLS = 112 * 128
BLOCKS = 4
GROUP = 16
BOTH = ("dp", "tensor")
VMEM = 16 * 1024 * 1024
SMALL = 10**5


def groups(count, steps):
    seen, found = set(), []
    for first in range(count):
        if first in seen:
            continue
        members = [first]
        for step in steps:
            members = members + [member ^ step for member in members]
        members = sorted(members)
        seen.update(members)
        found.append(members)
    return found


def exchange(pieces, axes, steps=None):
    members = None
    if steps is not None:
        members = groups(256 if axes == BOTH else 16, steps)
    return lax.all_to_all(pieces, axes, 0, 0, tiled=True, axis_index_groups=members)


def to_all(piece, count):
    return jnp.broadcast_to(piece[None], (count,) + piece.shape)


PLANE = (2, 4, 8, 16)
DEPTH = (2, 4, 8)


def gelu_pair(values):
    square = values * values
    inner = values * (gelu_scale + (gelu_scale * gelu_cubic) * square)
    tanh_part = jnp.tanh(inner)
    above = 1.0 + tanh_part
    act = values * above
    slope = above + act * (1.0 - tanh_part) * (
        gelu_scale + (3.0 * gelu_scale * gelu_cubic) * square
    )
    return act, slope


stretch = (gelu_scale * gelu_cubic) ** (1.0 / 3.0)


def stretched_gelu_pair(values):
    base = values * values + gelu_scale / stretch
    tanh_part = jnp.tanh(values * base)
    above = 1.0 + tanh_part
    act = values * above
    slope = above + act * (1.0 - tanh_part) * (3.0 * base - 2.0 * gelu_scale / stretch)
    return act, slope


def params(**more):
    return pltpu.CompilerParams(vmem_limit_bytes=VMEM, **more)


def cost(flops, size):
    return pl.CostEstimate(flops=flops, bytes_accessed=size, transcendentals=0)


def join_low(first, second, low):
    return jnp.where(low, first, pltpu.roll(second, 64, 1))


def join_high(first, second, low):
    return jnp.where(low, pltpu.roll(first, 64, 1), second)


def full(*shape):
    return pl.BlockSpec(shape, lambda *unused: (0,) * len(shape))


def in_vmem(count):
    return [pl.BlockSpec(memory_space=pltpu.VMEM)] * count


def in_hbm(count):
    return [pl.BlockSpec(memory_space=pltpu.HBM)] * count


def held(shape, kind):
    return pltpu.VMEM(shape, kind)


def kept(*arrays):
    return [pltpu.with_memory_space_constraint(array, pltpu.VMEM) for array in arrays]


def far_memory(*arrays):
    return [pltpu.with_memory_space_constraint(array, pltpu.HBM) for array in arrays]


def tensor_place():
    place = lax.axis_index("tensor")
    return lax.rem(place, 2), lax.div(place, 2)


def image_place():
    image = lax.axis_index("dp")
    return lax.div(image, 2), lax.rem(image, 2)


def lanes_of(shape):
    return lax.broadcasted_iota(jnp.int32, shape, 1)


def down_rows(row):
    return jnp.broadcast_to(row, (128, 128)).T


def start_kernel(
    x, c, w_expand, w_project, dw_rows, se_down, se_up,
    packed, edge,
    tall, wide, expand_in, project_in, dw_in, down_in, up_in, sems,
):
    core, _ = tensor_place()
    z, yh = image_place()
    pairs = (
        (w_expand, expand_in),
        (w_project, project_in),
        (dw_rows, dw_in),
        (se_down, down_in),
        (se_up, up_in),
        (x.at[pl.ds(5 * core, 2)], edge.at[0]),
        (c.at[pl.ds(5 * core, 2)], edge.at[1]),
    )
    copies = [pltpu.make_async_copy(a, b, sems.at[i]) for i, (a, b) in enumerate(pairs)]
    for copy in copies:
        copy.start()
    wide[0:16, :] = jnp.zeros((16, 128), f32)
    for copy in copies[:5]:
        copy.wait()
    wide[0:9, 0:64] = dw_in[...].astype(f32)
    tall[0:64, 0:64] = down_in[...].astype(f32)
    tall[0:64, 64:128] = up_in[...].astype(f32)
    wide[16:32, 0:64] = expand_in[...].astype(f32)
    wide[16:32, 64:128] = project_in[...].astype(f32)
    squeeze_rows = tall[pl.ds(yh * 32 + z * 4, 4), :]
    tap_row = wide[pl.ds(yh * 8 + z, 1), :]
    tall[16:32, :] = jnp.zeros((16, 128), f32)
    tall[16:20, :] = squeeze_rows
    tall[20:21, :] = tap_row
    piece = jnp.concatenate([wide[16:32, :], tall[16:32, :]], axis=0).astype(bf16)
    for other in range(8):
        packed[other] = piece
    for copy in copies[5:]:
        copy.wait()


def start(x, c, w_expand, w_project, dw_rows, se_down, se_up):
    return pl.pallas_call(
        start_kernel,
        in_specs=in_hbm(7),
        out_specs=in_vmem(2),
        out_shape=[
            jax.ShapeDtypeStruct((8, 32, 128), bf16),
            held((2, 2, 1, CH, COLS), bf16),
        ],
        scratch_shapes=[
            pltpu.VMEM((64, 128), f32),
            pltpu.VMEM((32, 128), f32),
            pltpu.VMEM((16, 64), bf16),
            pltpu.VMEM((16, 64), bf16),
            pltpu.VMEM((9, 64), bf16),
            pltpu.VMEM((64, 64), bf16),
            pltpu.VMEM((64, 64), bf16),
            pltpu.SemaphoreType.DMA((7,)),
        ],
        compiler_params=params(),
        cost_estimate=cost(SMALL, SMALL),
        name="start",
    )(*far_memory(x, c, w_expand, w_project, dw_rows, se_down, se_up))


def spread_kernel(lines, after, out, squeeze_rows, tap_rows):
    tap_rows[...] = jnp.zeros((16, 128), f32)
    for z in range(8):
        small = lines[z, 16:32, :].astype(f32)
        squeeze_rows[z * 4 : z * 4 + 4, :] = small[0:4]
        tap_rows[z : z + 1, :] = small[4:5]
    squeeze_piece = squeeze_rows[...].astype(bf16)
    tap_piece = tap_rows[...].astype(bf16)
    for other in range(16):
        for z in range(8):
            out[other, z] = lines[z, 0:16, :]
        out[other, 8] = squeeze_piece[0:16]
        out[other, 9] = squeeze_piece[16:32]
        out[other, 10] = tap_piece


def spread(lines, after):
    return pl.pallas_call(
        spread_kernel,
        in_specs=in_vmem(2),
        out_specs=in_vmem(1)[0],
        out_shape=jax.ShapeDtypeStruct((16, 11, 16, 128), bf16),
        scratch_shapes=[pltpu.VMEM((32, 128), f32), pltpu.VMEM((16, 128), f32)],
        compiler_params=params(),
        cost_estimate=cost(SMALL, SMALL),
        name="spread",
    )(lines, after)


def normal_of(x):
    values = x.astype(f32)
    center = values - jnp.mean(values, axis=0, keepdims=True)
    inv_std = lax.rsqrt(jnp.mean(center * center, axis=0, keepdims=True) + 1e-05)
    return (center * inv_std).astype(bf16)


def lane_block(row):
    return pl.ds(pl.multiple_of(row * 128, 128), 128)


def copy_all(pairs, sems):
    copies = [pltpu.make_async_copy(a, b, sems.at[i]) for i, (a, b) in enumerate(pairs)]
    for copy in copies:
        copy.start()
    return copies


def main_norm_kernel(own_x, other_x, normed_out, done, own_x_in, other_x_in, normed, sems):
    done[...] = jnp.zeros((8, 128), f32)
    core, _ = tensor_place()
    copies = copy_all(((own_x, own_x_in), (other_x, other_x_in)), sems)
    sent = []
    for i, (x, first) in enumerate(((own_x_in, 7 * core), (other_x_in, 7 - 7 * core))):
        copies[i].wait()
        for row in range(7):
            normed[i, :, row * 128 : row * 128 + 128] = normal_of(x[row, 0])
        part = pl.ds(pl.multiple_of(first * 128, 7 * 128), 7 * 128)
        sent.append(pltpu.make_async_copy(normed.at[i], normed_out.at[:, part], sems.at[i]))
        sent[i].start()
    for copy in sent:
        copy.wait()


def main_norm(own_x, other_x):
    return pl.pallas_call(
        main_norm_kernel,
        in_specs=in_hbm(2),
        out_specs=in_hbm(1) + in_vmem(1),
        out_shape=[
            pltpu.HBM((CH, ROWS * COLS), bf16),
            jax.ShapeDtypeStruct((8, 128), f32),
        ],
        scratch_shapes=[pltpu.VMEM((7, 1, CH, COLS), bf16)] * 2
        + [pltpu.VMEM((2, CH, 7 * COLS), bf16), pltpu.SemaphoreType.DMA((2,))],
        compiler_params=params(),
        cost_estimate=cost(SMALL, SMALL),
        name="main_norm",
    )(*far_memory(own_x, other_x))


def edge_norm_kernel(near, after, edge_out, done, edge, sem):
    done[...] = after[...]
    for row in range(2):
        edge[0, :, row * 128 : row * 128 + 128] = normal_of(near[0, row, 0])
        edge[1, :, row * 128 : row * 128 + 128] = near[1, row, 0]
    copy = pltpu.make_async_copy(edge, edge_out, sem)
    copy.start()
    copy.wait()


def edge_norm(near, after):
    return pl.pallas_call(
        edge_norm_kernel,
        in_specs=in_vmem(2),
        out_specs=in_hbm(1) + in_vmem(1),
        out_shape=[pltpu.HBM((2, CH, 2 * COLS), bf16), jax.ShapeDtypeStruct((8, 128), f32)],
        scratch_shapes=[
            pltpu.VMEM((2, CH, 2 * COLS), bf16),
            pltpu.SemaphoreType.DMA,
        ],
        compiler_params=params(),
        cost_estimate=cost(SMALL, SMALL),
        name="edge_norm",
    )(near, after)


def spread_taps(sources, taps, place, turned, scale):
    low = lanes_of((16, 128)) < 64
    early = join_low(sources[0][0].astype(f32), sources[0][1].astype(f32), low)
    late = join_low(sources[1][0].astype(f32), sources[1][1].astype(f32), low)
    early = early * scale
    late = late * scale
    lane = lanes_of((128, 128))
    for tap in range(9):
        spread = down_rows(early[tap : tap + 1, :] if tap < 8 else late[0:1, :])
        if tap % 3 == (2 if turned else 0):
            spread = jnp.where(lane == 0, 0.0, spread)
        if tap % 3 == (0 if turned else 2):
            spread = jnp.where(lane == 127, 0.0, spread)
        taps[tap, place : place + 128, :] = spread


def forward_kernel(
    weights, normed_in, near_in, far_in, own_c, other_c,
    normed, act1, slope1, act2, slope2, grad_hidden, proj_grad, w_exp, w_proj, squeeze_rows, sums,
    cot, own_c_in, other_c_in, near, far, expanded, taps, pool, gate, sems,
):
    core, chip = tensor_place()
    copies = copy_all(
        (
            (near_in, near),
            (far_in, far),
            (normed_in, normed),
            (own_c, own_c_in),
            (other_c, other_c_in),
        ),
        sems,
    )
    low = lanes_of((16, 128)) < 64
    for block in range(BLOCKS):
        cells = slice(block * 128, block * 128 + 128)
        for z in range(8):
            for yh in range(2):
                first = weights[yh, 2 * block, z].astype(f32)
                second = weights[yh, 2 * block + 1, z].astype(f32)
                rows = slice((z * 2 + yh) * 16, (z * 2 + yh) * 16 + 16)
                w_exp[rows, cells] = join_low(first, second, low).astype(bf16)
                w_proj[rows, cells] = join_high(first, second, low).astype(bf16)
        spread_taps(
            [[weights[yh, 2 * block + j, 10] for j in range(2)] for yh in range(2)],
            taps,
            block * 128,
            False,
            0.5 * stretch,
        )
    squeeze_rows[...] = weights[:, :, 8:10]

    def multiply(weight, source, target, place):
        target[:, place * 128 : place * 128 + source.shape[1]] = lax.dot_general(
            weight[...], source, (((0,), (0,)), ((), ())), preferred_element_type=f32
        ).astype(target.dtype)

    for copy in copies[:3]:
        copy.wait()
    near_first = core == 0
    multiply(w_exp, jnp.where(near_first, near[0], far[0]), expanded, 0)
    multiply(w_exp, jnp.where(near_first, far[0], near[0]), expanded, ROWS + 2)
    above = jnp.where(near_first, near[1, :, 128:256], far[1, :, 128:256])
    below = jnp.where(near_first, far[1, :, 0:128], near[1, :, 0:128])
    multiply(w_proj, above, grad_hidden, 0)
    multiply(w_proj, below, grad_hidden, ROWS + 1)
    for part in range(ROWS // 2):
        cells = slice(part * 256, part * 256 + 256)
        multiply(w_exp, normed[:, cells], expanded, 2 + 2 * part)
    for copy, c, first in ((copies[3], own_c_in, 7 * core), (copies[4], other_c_in, 7 - 7 * core)):
        copy.wait()
        for row in range(7):
            cot[:, lane_block(first + row)] = c[row, 0]
    for part in range(ROWS // 2):
        cells = slice(part * 256, part * 256 + 256)
        multiply(w_proj, cot[:, cells], grad_hidden, 1 + 2 * part)
    first_chip = jnp.where(chip > 0, 1.0, 0.0)
    last_chip = jnp.where(chip < 7, 1.0, 0.0)

    def one_group(index, carry):
        rows = pl.ds(pl.multiple_of(index * GROUP, GROUP), GROUP)
        tap = [taps[k, rows, :] for k in range(9)]
        running = {}
        pool_sum = jnp.zeros((GROUP, COLS), f32)
        gate_sum = jnp.zeros((GROUP, COLS), f32)
        for h in range(EXT):
            act, slope = gelu_pair(expanded[rows, h * 128 : h * 128 + 128])
            act1[rows, h * 128 : h * 128 + 128] = act.astype(bf16)
            if 2 <= h < ROWS + 2:
                slope1[rows, (h - 2) * 128 : (h - 1) * 128] = slope.astype(bf16)
            left = pltpu.roll(act, 1, 1)
            right = pltpu.roll(act, 127, 1)
            for i in range(3):
                m = h + 1 - i
                if not 1 <= m <= ROWS + 2:
                    continue
                term = tap[3 * i] * left + tap[3 * i + 1] * act + tap[3 * i + 2] * right
                running[m] = running[m] + term if m in running else term
            m = h - 1
            if not 1 <= m <= ROWS + 2:
                continue
            act, slope = stretched_gelu_pair(running.pop(m))
            if m == 1:
                slope = slope * first_chip
            if m == ROWS + 2:
                slope = slope * last_chip
            slope2[rows, (m - 1) * 128 : m * 128] = slope.astype(bf16)
            if 2 <= m < ROWS + 2:
                act2[rows, (m - 2) * 128 : (m - 1) * 128] = act.astype(bf16)
                pool_sum = pool_sum + act
                grad = grad_hidden[rows, (m - 1) * 128 : m * 128].astype(f32)
                gate_sum = gate_sum + act * grad
        pool[rows, :] = pool_sum
        gate[rows, :] = gate_sum
        return carry

    lax.fori_loop(0, HALF // GROUP, one_group, 0, unroll=2)
    for block in range(BLOCKS):
        cells = slice(block * 128, block * 128 + 128)
        pool_row = jnp.sum(pool[cells, :].T, axis=0, keepdims=True) * (0.5 / stretch)
        gate_row = jnp.sum(gate[cells, :].T, axis=0, keepdims=True) * (0.5 / stretch)
        for other in range(16):
            sums[other, block : block + 1, :] = pool_row
            sums[other, BLOCKS + block : BLOCKS + block + 1, :] = gate_row
    proj_grad[...] = lax.dot_general(
        cot[...], act2[...], (((1,), (1,)), ((), ())), preferred_element_type=f32
    )


def forward(weights, normed, near, far, own_c, other_c):
    return pl.pallas_call(
        forward_kernel,
        in_specs=in_vmem(1) + in_hbm(5),
        out_specs=in_vmem(11),
        scratch_shapes=[
            pltpu.VMEM((CH, ROWS * COLS), bf16),
            pltpu.VMEM((7, 1, CH, COLS), bf16),
            pltpu.VMEM((7, 1, CH, COLS), bf16),
            pltpu.VMEM((2, CH, 2 * COLS), bf16),
            pltpu.VMEM((2, CH, 2 * COLS), bf16),
            pltpu.VMEM((HALF, EXT * COLS), f32),
            pltpu.VMEM((9, HALF, 128), f32),
            pltpu.VMEM((HALF, 128), f32),
            pltpu.VMEM((HALF, 128), f32),
            pltpu.SemaphoreType.DMA((5,)),
        ],
        out_shape=[
            held((CH, ROWS * COLS), bf16),
            held((HALF, EXT * COLS), bf16),
            held((HALF, ROWS * COLS), bf16),
            held((HALF, ROWS * COLS), bf16),
            held((HALF, (ROWS + 2) * COLS), bf16),
            held((HALF, (ROWS + 2) * COLS), bf16),
            held((CH, HALF), f32),
            held((CH, HALF), bf16),
            held((CH, HALF), bf16),
            held((2, 8, 2, 16, 128), bf16),
            jax.ShapeDtypeStruct((16, 8, 128), f32),
        ],
        compiler_params=params(),
        cost_estimate=cost(10**9, 50 * 10**6),
        name="forward",
    )(weights, *far_memory(normed, near, far, own_c, other_c))


def excite_kernel(sums, own_rows, other_rows, coef):
    low = lanes_of((SQ, 128)) < 64
    totals = []
    for half in range(2):
        total = sums[half]
        for other in range(1, 8):
            total = total + sums[2 * other + half]
        totals.append(total)
    core, _ = tensor_place()
    is_first = core == 0
    ordered = (
        jnp.where(is_first, totals[0], totals[1]),
        jnp.where(is_first, totals[1], totals[0]),
    )
    pooled, grad_gate, down, up = [], [], [], []
    for total, rows in zip(ordered, (own_rows, other_rows)):
        for block in range(BLOCKS):
            pooled.append(total[block : block + 1] * (1.0 / CELLS))
            grad_gate.append(total[BLOCKS + block : BLOCKS + block + 1])
            halves = [
                jnp.concatenate(
                    [rows[yh, 2 * block + j, part].astype(f32) for yh in range(2) for part in range(2)],
                    axis=0,
                )
                for j in range(2)
            ]
            down.append(join_low(halves[0], halves[1], low))
            up.append(join_high(halves[0], halves[1], low))
    count = 2 * BLOCKS
    squeeze = sum(jnp.sum(down[b] * pooled[b], axis=1, keepdims=True) for b in range(count))
    sig = 1.0 / (1.0 + jnp.exp(-squeeze))
    swish = squeeze * sig
    gating, grad_excite = [], []
    for b in range(count):
        logit = jnp.sum(up[b] * swish, axis=0, keepdims=True)
        gating.append(1.0 / (1.0 + jnp.exp(-logit)))
        grad_excite.append(grad_gate[b] * gating[b] * (1.0 - gating[b]))
    grad_swish = sum(jnp.sum(up[b] * grad_excite[b], axis=1, keepdims=True) for b in range(count))
    grad_squeeze = grad_swish * sig * (1.0 + squeeze * (1.0 - sig))
    side = jnp.concatenate([swish, grad_squeeze], axis=0)
    side_row = jnp.broadcast_to(side, (128, 128)).T[0:1, :]
    for b in range(BLOCKS):
        cells = slice(b * 128, b * 128 + 128)
        grad_pooled = jnp.sum(down[b] * grad_squeeze, axis=0, keepdims=True)
        coef[0:1, cells] = gating[b]
        coef[1:2, cells] = grad_pooled * (1.0 / CELLS)
        coef[2:3, cells] = pooled[b]
        coef[3:4, cells] = grad_excite[b]
        coef[4:5, cells] = side_row
    coef[5:8, :] = jnp.zeros((3, HALF), f32)


def excite(sums, own_rows, other_rows):
    return pl.pallas_call(
        excite_kernel,
        in_specs=in_vmem(3),
        out_specs=in_vmem(1)[0],
        out_shape=held((8, HALF), f32),
        compiler_params=params(),
        cost_estimate=cost(SMALL, 4 * 10**6),
        name="excite",
    )(sums, *kept(own_rows), other_rows)


def backward_kernel(
    coef, weights, normed, act1, slope1, slope2, grad_hidden, proj_grad, w_proj, w_exp, act2,
    grad_out, pieces_out, other_out,
    grad_expanded, pieces, other, copied, pieces_copied, other_copied,
    taps, gates, pools, kernel_sums, tap_rows,
):
    for block in range(BLOCKS):
        cells = slice(block * 128, block * 128 + 128)
        spread_taps(
            [[weights[yh, 2 * block + j, 10] for j in range(2)] for yh in range(2)],
            taps,
            block * 128,
            True,
            0.5,
        )
        gates[cells, :] = down_rows(coef[0:1, cells] * 0.5)
        pools[cells, :] = down_rows(coef[1:2, cells] * 0.5)
    core, _ = tensor_place()
    cells = pl.ds(pl.multiple_of((1 - core) * (7 * COLS), 7 * COLS), 7 * COLS)
    gated = (w_proj[...].astype(f32) * (coef[0:1, :] * (0.5 / stretch))).astype(bf16)
    projected = jnp.dot(gated, act2[:, cells], preferred_element_type=f32).astype(bf16)
    for row in range(7):
        other[0, row] = projected[:, row * 128 : row * 128 + 128]
    other_copies = [
        pltpu.make_async_copy(other.at[i], other_out.at[i], other_copied.at[i]) for i in range(2)
    ]
    other_copies[0].start()
    lane = lanes_of((GROUP, COLS))

    def one_group(index, carry):
        rows = pl.ds(pl.multiple_of(index * GROUP, GROUP), GROUP)
        tap = [taps[k, rows, :] for k in range(9)]
        gating = gates[rows, :]
        pooled = pools[rows, :]
        running = {}
        acts = {}
        sums = [None] * 9
        for m in range(1, ROWS + 3):
            cells = slice((m - 1) * 128, m * 128)
            grad = grad_hidden[rows, cells].astype(f32) * gating + pooled
            grad = grad * slope2[rows, cells].astype(f32)
            turned = (pltpu.roll(grad, 127, 1), grad, pltpu.roll(grad, 1, 1))
            for h in ((1, 2) if m == 1 else (m + 1,)):
                if h <= ROWS + 2:
                    acts[h] = act1[rows, h * 128 : h * 128 + 128].astype(f32)
            for i in range(3):
                h = m + i - 1
                if 2 <= h < ROWS + 2:
                    term = tap[3 * i] * turned[0] + tap[3 * i + 1] * turned[1] + tap[3 * i + 2] * turned[2]
                    running[h] = running[h] + term if h in running else term
                if 2 <= m < ROWS + 2:
                    for j in range(3):
                        term = turned[j] * acts[h]
                        k = 3 * i + j
                        sums[k] = term if sums[k] is None else sums[k] + term
            h = m - 1
            if 2 <= h < ROWS + 2:
                out = slice((h - 2) * 128, (h - 1) * 128)
                grad_expanded[rows, out] = (running.pop(h) * slope1[rows, out].astype(f32)).astype(bf16)
        for k in range(9):
            total = sums[k] * 0.5
            if k % 3 == 0:
                total = jnp.where(lane == 127, 0.0, total)
            if k % 3 == 2:
                total = jnp.where(lane == 0, 0.0, total)
            kernel_sums[k, rows, :] = total
        return carry

    def block_copy(block):
        rows = pl.ds(pl.multiple_of(block * 128, 128), 128)
        return pltpu.make_async_copy(grad_expanded.at[rows], grad_out.at[rows], copied.at[block])

    def one_block(block, carry):
        first = block * (128 // GROUP)
        lax.fori_loop(0, 128 // GROUP, lambda i, c: one_group(first + i, c), 0, unroll=2)
        block_copy(block).start()
        return carry

    lax.fori_loop(0, BLOCKS, one_block, 0)
    grad = jnp.dot(w_exp[...], grad_expanded[:, cells], preferred_element_type=f32).astype(bf16)
    for row in range(7):
        other[1, row] = grad[:, row * 128 : row * 128 + 128]
    other_copies[1].start()
    exp_grad = lax.dot_general(
        normed[...], grad_expanded[...], (((1,), (1,)), ((), ())), preferred_element_type=f32
    )
    low = lanes_of((CH, 128)) < 64
    tap_low = lanes_of((1, 128)) < 64
    tap_rows[...] = jnp.zeros((16, 128), f32)

    def pieces_copy(block):
        part = pl.ds(2 * block, 2)
        return pltpu.make_async_copy(
            pieces.at[:, part], pieces_out.at[:, part], pieces_copied.at[block]
        )

    for block in range(BLOCKS):
        cells = slice(block * 128, block * 128 + 128)
        scaled = proj_grad[:, cells] * (coef[0:1, cells] * (0.5 / stretch))
        first = join_low(exp_grad[:, cells], scaled, low).astype(bf16)
        second = join_high(exp_grad[:, cells], scaled, low).astype(bf16)
        for k in range(9):
            tap_rows[k : k + 1, :] = jnp.sum(kernel_sums[k, cells, :].T, axis=0, keepdims=True)
        tap_rows[9:10, :] = join_low(coef[2:3, cells], coef[3:4, cells], tap_low)
        tap_rows[10:11, :] = coef[4:5, cells]
        first_taps = tap_rows[...].astype(bf16)
        tap_rows[0:9, :] = pltpu.roll(tap_rows[...], 64, 1)[0:9]
        tap_rows[9:10, :] = join_high(coef[2:3, cells], coef[3:4, cells], tap_low)
        second_taps = tap_rows[...].astype(bf16)
        for yh in range(2):
            for z in range(8):
                rows = slice((z * 2 + yh) * 16, (z * 2 + yh) * 16 + 16)
                pieces[yh, 2 * block, z] = first[rows]
                pieces[yh, 2 * block + 1, z] = second[rows]
            pieces[yh, 2 * block, 8] = first_taps
            pieces[yh, 2 * block + 1, 8] = second_taps
        pieces_copy(block).start()
    for block in range(BLOCKS):
        block_copy(block).wait()
        pieces_copy(block).wait()
    for copy in other_copies:
        copy.wait()


def backward(coef, weights, normed, act1, slope1, slope2, grad_hidden, proj_grad, w_proj, w_exp, act2):
    return pl.pallas_call(
        backward_kernel,
        in_specs=in_vmem(11),
        out_specs=in_hbm(3),
        scratch_shapes=[
            pltpu.VMEM((HALF, ROWS * COLS), bf16),
            pltpu.VMEM((2, 8, 9, 16, 128), bf16),
            pltpu.VMEM((2, 7, CH, COLS), bf16),
            pltpu.SemaphoreType.DMA((BLOCKS,)),
            pltpu.SemaphoreType.DMA((BLOCKS,)),
            pltpu.SemaphoreType.DMA((2,)),
            pltpu.VMEM((9, HALF, 128), f32),
            pltpu.VMEM((HALF, 128), f32),
            pltpu.VMEM((HALF, 128), f32),
            pltpu.VMEM((9, HALF, 128), f32),
            pltpu.VMEM((16, 128), f32),
        ],
        out_shape=[
            pltpu.HBM((HALF, ROWS * COLS), bf16),
            pltpu.HBM((2, 8, 9, 16, 128), bf16),
            pltpu.HBM((2, 7, CH, COLS), bf16),
        ],
        compiler_params=params(),
        cost_estimate=cost(10**9, 45 * 10**6),
        name="backward",
    )(
        *kept(
            coef, weights, normed, act1, slope1, slope2, grad_hidden, proj_grad, w_proj, w_exp, act2
        )
    )


def finish_kernel(coef, w_proj, w_exp, act2, grad_expanded, arrived, x, c, block_out, input_grad, done):
    core, _ = tensor_place()
    cells = pl.ds(pl.multiple_of(core * (7 * COLS), 7 * COLS), 7 * COLS)
    gated = (w_proj[...].astype(f32) * (coef[0:1, :] * (0.5 / stretch))).astype(bf16)
    done[...] = jnp.zeros((8, 128), f32)
    all_projected = jnp.dot(gated, act2[:, cells], preferred_element_type=f32)
    all_grad = jnp.dot(w_exp[...], grad_expanded[:, cells], preferred_element_type=f32)
    for row in range(7):
        projected = all_projected[:, row * 128 : row * 128 + 128] + arrived[0, row].astype(f32)
        values = x[row, 0].astype(f32)
        block_out[row, 0] = (values + projected).astype(bf16)
        grad = all_grad[:, row * 128 : row * 128 + 128] + arrived[1, row].astype(f32)
        center = values - jnp.mean(values, axis=0, keepdims=True)
        inv_std = lax.rsqrt(jnp.mean(center * center, axis=0, keepdims=True) + 1e-05)
        normal = center * inv_std
        mean_grad = jnp.mean(grad, axis=0, keepdims=True)
        mean_inner = jnp.mean(grad * normal, axis=0, keepdims=True)
        input_grad[row, 0] = (
            c[row, 0].astype(f32) + inv_std * (grad - mean_grad - normal * mean_inner)
        ).astype(bf16)


def finish(coef, w_proj, w_exp, act2, grad_expanded, arrived, x, c):
    return pl.pallas_call(
        finish_kernel,
        in_specs=in_vmem(8),
        out_specs=in_vmem(3),
        out_shape=[
            jax.ShapeDtypeStruct((7, 1, CH, COLS), bf16),
            jax.ShapeDtypeStruct((7, 1, CH, COLS), bf16),
            jax.ShapeDtypeStruct((8, 128), f32),
        ],
        compiler_params=params(),
        cost_estimate=cost(SMALL, SMALL),
        name="finish",
    )(*kept(coef, w_proj, w_exp, act2), grad_expanded, arrived, x, c)


def middle_kernel(pieces, after, out):
    for slot in range(9):
        total = pieces[0, slot].astype(f32)
        for other in range(1, 16):
            total = total + pieces[other, slot].astype(f32)
        total = total.astype(bf16)
        if slot < 8:
            out[slot, 0] = total
        else:
            for z in range(8):
                out[z, 1] = total
    low = lanes_of((SQ, 128)) < 64
    outer = jnp.zeros((SQ, 128), f32)
    for yh in range(2):
        vectors = pieces[yh * 8, 8].astype(f32)
        column = down_rows(vectors[10:11, :])
        outer = outer + jnp.where(low, column[64:128], column[0:64]) * vectors[9:10, :]
    outer = outer.astype(bf16)
    for z in range(8):
        for part in range(4):
            out[z, 2 + part] = outer[part * 16 : part * 16 + 16]


def middle(pieces, after):
    return pl.pallas_call(
        middle_kernel,
        in_specs=in_vmem(2),
        out_specs=in_vmem(1)[0],
        out_shape=jax.ShapeDtypeStruct((8, 6, 16, 128), bf16),
        compiler_params=params(),
        cost_estimate=cost(10**6, 4 * 10**6),
        name="middle",
    )(pieces, after)


def tail_kernel(lines, exp_grad, proj_grad, kernel_grad, down_grad, up_grad):
    def total_of(slot):
        total = lines[0, slot].astype(f32)
        for z in range(1, 8):
            total = total + lines[z, slot].astype(f32)
        return total

    first = total_of(0)
    exp_grad[...] = first[:, 0:64]
    proj_grad[...] = pltpu.roll(first, 64, 1)[:, 0:64]
    kernel_grad[...] = total_of(1)[0:9, 0:64]
    for part in range(4):
        both = total_of(2 + part)
        down_grad[part * 16 : part * 16 + 16, :] = both[:, 0:64]
        up_grad[part * 16 : part * 16 + 16, :] = pltpu.roll(both, 64, 1)[:, 0:64]


def tail(lines):
    return pl.pallas_call(
        tail_kernel,
        in_specs=in_vmem(1),
        out_specs=in_vmem(5),
        out_shape=[
            jax.ShapeDtypeStruct((16, 64), f32),
            jax.ShapeDtypeStruct((16, 64), f32),
            jax.ShapeDtypeStruct((9, 64), f32),
            jax.ShapeDtypeStruct((64, 64), f32),
            jax.ShapeDtypeStruct((64, 64), f32),
        ],
        compiler_params=params(),
        cost_estimate=cost(10**6, 2 * 10**6),
        name="tail",
    )(lines)


def body(inputs, cotangent, w_expand, w_project, dw_kernel, se_down, se_up):
    swap = [(i, i ^ 1) for i in range(16)]
    edges = [(i, i + 1) for i in range(1, 14, 2)] + [(i + 1, i) for i in range(1, 14, 2)]
    packed, edge = start(inputs, cotangent, w_expand, w_project, dw_kernel.T, se_down, se_up)
    with jax.named_scope("rows"):
        near = lax.ppermute(edge, "tensor", edges)
        other_x = lax.ppermute(inputs, "tensor", swap)
        other_c = lax.ppermute(cotangent, "tensor", swap)
        normed, main_done = main_norm(inputs, other_x)
        near, edge_done = edge_norm(near, main_done)
        far = lax.ppermute(near, "tensor", swap)
    with jax.named_scope("weights"):
        lines = exchange(packed, "dp", DEPTH)
        copies = spread(lines, edge_done)
        weights = exchange(copies, BOTH, PLANE).reshape(2, 8, 11, 16, 128)
    (
        normed, act1, slope1, act2, slope2, grad_hidden, proj_grad, w_exp, w_proj, own_rows, sums
    ) = forward(weights, normed, near, far, cotangent, other_c)
    with jax.named_scope("sums"):
        other_rows = lax.ppermute(own_rows, "tensor", swap)
        all_sums = exchange(sums, "tensor")
    coef = excite(all_sums, own_rows, other_rows)
    grad_expanded, pieces, partial_out = backward(
        coef, weights, normed, act1, slope1, slope2, grad_hidden, proj_grad, w_proj, w_exp, act2
    )
    with jax.named_scope("finish"):
        arrived = lax.ppermute(partial_out, "tensor", swap)
        block_out, input_grad, done = finish(
            coef, w_proj, w_exp, act2, grad_expanded, arrived, inputs, cotangent
        )
    with jax.named_scope("gradients"):
        pieces = exchange(pieces.reshape(16, 9, 16, 128), BOTH, PLANE)
        lines = exchange(middle(pieces, done), "dp", DEPTH)
        exp_grad, proj_grad, kernel_grad, down_grad, up_grad = tail(lines)
    return (block_out, input_grad, exp_grad, proj_grad, kernel_grad.T, down_grad, up_grad)


def solution(mesh):
    placed = (
        P("tensor", "dp", None, None),
        P("tensor", "dp", None, None),
        P("dp", "tensor"),
        P("dp", "tensor"),
        P("tensor", None),
        P(None, "tensor"),
        P(None, "tensor"),
    )
    return jax.shard_map(
        body,
        mesh=mesh,
        in_specs=placed,
        out_specs=(
            P("tensor", "dp", None, None),
            P("tensor", "dp", None, None),
            P("dp", "tensor"),
            P("dp", "tensor"),
            P("tensor", None),
            P(None, "tensor"),
            P(None, "tensor"),
        ),
        check_vma=False,
    )
```

```python
import jax
import jax.numpy as jnp
from jax import lax
from jax.experimental import pallas as pl
from jax.experimental.pallas import tpu as pltpu
from jax.sharding import PartitionSpec as P

bf16 = jnp.bfloat16
f32 = jnp.float32

gelu_scale = 0.7978845608
gelu_cubic = 0.044715

CH = 256
HALF = 512
SQ = 64
COLS = 128
ROWS = 14
EXT = ROWS + 4
CELLS = 112 * 128
BLOCKS = 4
GROUP = 16
BOTH = ("dp", "tensor")
VMEM = 16 * 1024 * 1024
SMALL = 10**5


def groups(count, steps):
    seen, found = set(), []
    for first in range(count):
        if first in seen:
            continue
        members = [first]
        for step in steps:
            members = members + [member ^ step for member in members]
        members = sorted(members)
        seen.update(members)
        found.append(members)
    return found


def exchange(pieces, axes, steps=None):
    members = None
    if steps is not None:
        members = groups(256 if axes == BOTH else 16, steps)
    return lax.all_to_all(pieces, axes, 0, 0, tiled=True, axis_index_groups=members)


def to_all(piece, count):
    return jnp.broadcast_to(piece[None], (count,) + piece.shape)


PLANE = (2, 4, 8, 16)
DEPTH = (2, 4, 8)


def gelu_pair(values):
    square = values * values
    inner = values * (gelu_scale + (gelu_scale * gelu_cubic) * square)
    tanh_part = jnp.tanh(inner)
    above = 1.0 + tanh_part
    act = values * above
    slope = above + act * (1.0 - tanh_part) * (
        gelu_scale + (3.0 * gelu_scale * gelu_cubic) * square
    )
    return act, slope


stretch = (gelu_scale * gelu_cubic) ** (1.0 / 3.0)


def stretched_gelu_pair(values):
    base = values * values + gelu_scale / stretch
    tanh_part = jnp.tanh(values * base)
    above = 1.0 + tanh_part
    act = values * above
    slope = above + act * (1.0 - tanh_part) * (3.0 * base - 2.0 * gelu_scale / stretch)
    return act, slope


def params(**more):
    return pltpu.CompilerParams(vmem_limit_bytes=VMEM, **more)


def cost(flops, size):
    return pl.CostEstimate(flops=flops, bytes_accessed=size, transcendentals=0)


def join_low(first, second, low):
    return jnp.where(low, first, pltpu.roll(second, 64, 1))


def join_high(first, second, low):
    return jnp.where(low, pltpu.roll(first, 64, 1), second)


def full(*shape):
    return pl.BlockSpec(shape, lambda *unused: (0,) * len(shape))


def in_vmem(count):
    return [pl.BlockSpec(memory_space=pltpu.VMEM)] * count


def in_hbm(count):
    return [pl.BlockSpec(memory_space=pltpu.HBM)] * count


def held(shape, kind):
    return pltpu.VMEM(shape, kind)


def kept(*arrays):
    return [pltpu.with_memory_space_constraint(array, pltpu.VMEM) for array in arrays]


def far_memory(*arrays):
    return [pltpu.with_memory_space_constraint(array, pltpu.HBM) for array in arrays]


def tensor_place():
    place = lax.axis_index("tensor")
    return lax.rem(place, 2), lax.div(place, 2)


def image_place():
    image = lax.axis_index("dp")
    return lax.div(image, 2), lax.rem(image, 2)


def lanes_of(shape):
    return lax.broadcasted_iota(jnp.int32, shape, 1)


def down_rows(row):
    return jnp.broadcast_to(row, (128, 128)).T


def start_kernel(
    x, c, w_expand, w_project, dw_rows, se_down, se_up,
    packed, edge,
    tall, wide, expand_in, project_in, dw_in, down_in, up_in, sems,
):
    core, _ = tensor_place()
    z, yh = image_place()
    pairs = (
        (w_expand, expand_in),
        (w_project, project_in),
        (dw_rows, dw_in),
        (se_down, down_in),
        (se_up, up_in),
        (x.at[pl.ds(5 * core, 2)], edge.at[0]),
        (c.at[pl.ds(5 * core, 2)], edge.at[1]),
    )
    copies = [pltpu.make_async_copy(a, b, sems.at[i]) for i, (a, b) in enumerate(pairs)]
    for copy in copies:
        copy.start()
    wide[0:16, :] = jnp.zeros((16, 128), f32)
    for copy in copies[:5]:
        copy.wait()
    wide[0:9, 0:64] = dw_in[...].astype(f32)
    tall[0:64, 0:64] = down_in[...].astype(f32)
    tall[0:64, 64:128] = up_in[...].astype(f32)
    wide[16:32, 0:64] = expand_in[...].astype(f32)
    wide[16:32, 64:128] = project_in[...].astype(f32)
    squeeze_rows = tall[pl.ds(yh * 32 + z * 4, 4), :]
    tap_row = wide[pl.ds(yh * 8 + z, 1), :]
    tall[16:32, :] = jnp.zeros((16, 128), f32)
    tall[16:20, :] = squeeze_rows
    tall[20:21, :] = tap_row
    piece = jnp.concatenate([wide[16:32, :], tall[16:32, :]], axis=0).astype(bf16)
    for other in range(8):
        packed[other] = piece
    for copy in copies[5:]:
        copy.wait()


def start(x, c, w_expand, w_project, dw_rows, se_down, se_up):
    return pl.pallas_call(
        start_kernel,
        in_specs=in_hbm(7),
        out_specs=in_vmem(2),
        out_shape=[
            jax.ShapeDtypeStruct((8, 32, 128), bf16),
            held((2, 2, 1, CH, COLS), bf16),
        ],
        scratch_shapes=[
            pltpu.VMEM((64, 128), f32),
            pltpu.VMEM((32, 128), f32),
            pltpu.VMEM((16, 64), bf16),
            pltpu.VMEM((16, 64), bf16),
            pltpu.VMEM((9, 64), bf16),
            pltpu.VMEM((64, 64), bf16),
            pltpu.VMEM((64, 64), bf16),
            pltpu.SemaphoreType.DMA((7,)),
        ],
        compiler_params=params(),
        cost_estimate=cost(SMALL, SMALL),
        name="start",
    )(*far_memory(x, c, w_expand, w_project, dw_rows, se_down, se_up))


def spread_kernel(lines, after, out, squeeze_rows, tap_rows):
    tap_rows[...] = jnp.zeros((16, 128), f32)
    for z in range(8):
        small = lines[z, 16:32, :].astype(f32)
        squeeze_rows[z * 4 : z * 4 + 4, :] = small[0:4]
        tap_rows[z : z + 1, :] = small[4:5]
    squeeze_piece = squeeze_rows[...].astype(bf16)
    tap_piece = tap_rows[...].astype(bf16)
    for other in range(16):
        for z in range(8):
            out[other, z] = lines[z, 0:16, :]
        out[other, 8] = squeeze_piece[0:16]
        out[other, 9] = squeeze_piece[16:32]
        out[other, 10] = tap_piece


def spread(lines, after):
    return pl.pallas_call(
        spread_kernel,
        in_specs=in_vmem(2),
        out_specs=in_vmem(1)[0],
        out_shape=jax.ShapeDtypeStruct((16, 11, 16, 128), bf16),
        scratch_shapes=[pltpu.VMEM((32, 128), f32), pltpu.VMEM((16, 128), f32)],
        compiler_params=params(),
        cost_estimate=cost(SMALL, SMALL),
        name="spread",
    )(lines, after)


def normal_of(x):
    values = x.astype(f32)
    center = values - jnp.mean(values, axis=0, keepdims=True)
    inv_std = lax.rsqrt(jnp.mean(center * center, axis=0, keepdims=True) + 1e-05)
    return (center * inv_std).astype(bf16)


def lane_block(row):
    return pl.ds(pl.multiple_of(row * 128, 128), 128)


def copy_all(pairs, sems):
    copies = [pltpu.make_async_copy(a, b, sems.at[i]) for i, (a, b) in enumerate(pairs)]
    for copy in copies:
        copy.start()
    return copies


def main_norm_kernel(own_x, other_x, normed_out, done, own_x_in, other_x_in, normed, sems):
    done[...] = jnp.zeros((8, 128), f32)
    core, _ = tensor_place()
    copies = copy_all(((own_x, own_x_in), (other_x, other_x_in)), sems)
    sent = []
    for i, (x, first) in enumerate(((own_x_in, 7 * core), (other_x_in, 7 - 7 * core))):
        copies[i].wait()
        for row in range(7):
            normed[i, :, row * 128 : row * 128 + 128] = normal_of(x[row, 0])
        part = pl.ds(pl.multiple_of(first * 128, 7 * 128), 7 * 128)
        sent.append(pltpu.make_async_copy(normed.at[i], normed_out.at[:, part], sems.at[i]))
        sent[i].start()
    for copy in sent:
        copy.wait()


def main_norm(own_x, other_x):
    return pl.pallas_call(
        main_norm_kernel,
        in_specs=in_hbm(2),
        out_specs=in_hbm(1) + in_vmem(1),
        out_shape=[
            pltpu.HBM((CH, ROWS * COLS), bf16),
            jax.ShapeDtypeStruct((8, 128), f32),
        ],
        scratch_shapes=[pltpu.VMEM((7, 1, CH, COLS), bf16)] * 2
        + [pltpu.VMEM((2, CH, 7 * COLS), bf16), pltpu.SemaphoreType.DMA((2,))],
        compiler_params=params(),
        cost_estimate=cost(SMALL, SMALL),
        name="main_norm",
    )(*far_memory(own_x, other_x))


def edge_norm_kernel(near, after, edge_out, done, edge, sem):
    done[...] = after[...]
    for row in range(2):
        edge[0, :, row * 128 : row * 128 + 128] = normal_of(near[0, row, 0])
        edge[1, :, row * 128 : row * 128 + 128] = near[1, row, 0]
    copy = pltpu.make_async_copy(edge, edge_out, sem)
    copy.start()
    copy.wait()


def edge_norm(near, after):
    return pl.pallas_call(
        edge_norm_kernel,
        in_specs=in_vmem(2),
        out_specs=in_hbm(1) + in_vmem(1),
        out_shape=[pltpu.HBM((2, CH, 2 * COLS), bf16), jax.ShapeDtypeStruct((8, 128), f32)],
        scratch_shapes=[
            pltpu.VMEM((2, CH, 2 * COLS), bf16),
            pltpu.SemaphoreType.DMA,
        ],
        compiler_params=params(),
        cost_estimate=cost(SMALL, SMALL),
        name="edge_norm",
    )(near, after)


def spread_taps(sources, taps, place, turned, scale):
    low = lanes_of((16, 128)) < 64
    early = join_low(sources[0][0].astype(f32), sources[0][1].astype(f32), low)
    late = join_low(sources[1][0].astype(f32), sources[1][1].astype(f32), low)
    early = early * scale
    late = late * scale
    lane = lanes_of((128, 128))
    for tap in range(9):
        spread = down_rows(early[tap : tap + 1, :] if tap < 8 else late[0:1, :])
        if tap % 3 == (2 if turned else 0):
            spread = jnp.where(lane == 0, 0.0, spread)
        if tap % 3 == (0 if turned else 2):
            spread = jnp.where(lane == 127, 0.0, spread)
        taps[tap, place : place + 128, :] = spread


def forward_kernel(
    weights, normed_in, near_in, far_in, own_c, other_c,
    normed, act1, slope1, act2, slope2, grad_hidden, proj_grad, w_exp, w_proj, squeeze_rows, sums,
    cot, own_c_in, other_c_in, near, far, expanded, taps, sems,
):
    core, chip = tensor_place()
    copies = copy_all(
        (
            (near_in, near),
            (far_in, far),
            (normed_in, normed),
            (own_c, own_c_in),
            (other_c, other_c_in),
        ),
        sems,
    )
    low = lanes_of((16, 128)) < 64
    for block in range(BLOCKS):
        cells = slice(block * 128, block * 128 + 128)
        for z in range(8):
            for yh in range(2):
                first = weights[yh, 2 * block, z].astype(f32)
                second = weights[yh, 2 * block + 1, z].astype(f32)
                rows = slice((z * 2 + yh) * 16, (z * 2 + yh) * 16 + 16)
                w_exp[rows, cells] = join_low(first, second, low).astype(bf16)
                w_proj[rows, cells] = join_high(first, second, low).astype(bf16)
        spread_taps(
            [[weights[yh, 2 * block + j, 10] for j in range(2)] for yh in range(2)],
            taps,
            block * 128,
            False,
            0.5 * stretch,
        )
    squeeze_rows[...] = weights[:, :, 8:10]

    def multiply(weight, source, target, place):
        target[:, place * 128 : place * 128 + source.shape[1]] = lax.dot_general(
            weight[...], source, (((0,), (0,)), ((), ())), preferred_element_type=f32
        ).astype(target.dtype)

    for copy in copies[:3]:
        copy.wait()
    near_first = core == 0
    multiply(w_exp, jnp.where(near_first, near[0], far[0]), expanded, 0)
    multiply(w_exp, jnp.where(near_first, far[0], near[0]), expanded, ROWS + 2)
    for part in range(ROWS // 2):
        cells = slice(part * 256, part * 256 + 256)
        multiply(w_exp, normed[:, cells], expanded, 2 + 2 * part)
    first_chip = jnp.where(chip > 0, 1.0, 0.0)
    last_chip = jnp.where(chip < 7, 1.0, 0.0)

    def one_group(index, carry):
        rows = pl.ds(pl.multiple_of(index * GROUP, GROUP), GROUP)
        tap = [taps[k, rows, :] for k in range(9)]
        running = {}
        for h in range(EXT):
            act, slope = gelu_pair(expanded[rows, h * 128 : h * 128 + 128])
            act1[rows, h * 128 : h * 128 + 128] = act.astype(bf16)
            if 2 <= h < ROWS + 2:
                slope1[rows, (h - 2) * 128 : (h - 1) * 128] = slope.astype(bf16)
            left = pltpu.roll(act, 1, 1)
            right = pltpu.roll(act, 127, 1)
            for i in range(3):
                m = h + 1 - i
                if not 1 <= m <= ROWS + 2:
                    continue
                term = tap[3 * i] * left + tap[3 * i + 1] * act + tap[3 * i + 2] * right
                running[m] = running[m] + term if m in running else term
            m = h - 1
            if not 1 <= m <= ROWS + 2:
                continue
            act, slope = stretched_gelu_pair(running.pop(m))
            if m == 1:
                slope = slope * first_chip
            if m == ROWS + 2:
                slope = slope * last_chip
            slope2[rows, (m - 1) * 128 : m * 128] = slope.astype(bf16)
            if 2 <= m < ROWS + 2:
                act2[rows, (m - 2) * 128 : (m - 1) * 128] = act.astype(bf16)
        return carry

    lax.fori_loop(0, HALF // GROUP, one_group, 0, unroll=2)
    cot[CH : CH + 16, :] = jnp.ones((16, ROWS * COLS), bf16)
    for copy, c, first in ((copies[3], own_c_in, 7 * core), (copies[4], other_c_in, 7 - 7 * core)):
        copy.wait()
        for row in range(7):
            cot[0:CH, lane_block(first + row)] = c[row, 0]
    products = lax.dot_general(
        cot[...], act2[...], (((1,), (1,)), ((), ())), preferred_element_type=f32
    )
    proj_grad[...] = products[0:CH]
    pool = products[CH : CH + 1] * (0.5 / stretch)
    gate = jnp.sum(products[0:CH] * w_proj[...].astype(f32), axis=0, keepdims=True)
    gate = gate * (0.5 / stretch)
    for other in range(16):
        for block in range(BLOCKS):
            cells = slice(block * 128, block * 128 + 128)
            sums[other, block : block + 1, :] = pool[:, cells]
            sums[other, BLOCKS + block : BLOCKS + block + 1, :] = gate[:, cells]
    above = jnp.where(near_first, near[1, :, 128:256], far[1, :, 128:256])
    below = jnp.where(near_first, far[1, :, 0:128], near[1, :, 0:128])
    multiply(w_proj, above, grad_hidden, 0)
    multiply(w_proj, below, grad_hidden, ROWS + 1)
    for part in range(ROWS // 2):
        cells = slice(part * 256, part * 256 + 256)
        multiply(w_proj, cot[0:CH, cells], grad_hidden, 1 + 2 * part)


def forward(weights, normed, near, far, own_c, other_c):
    return pl.pallas_call(
        forward_kernel,
        in_specs=in_vmem(1) + in_hbm(5),
        out_specs=in_vmem(11),
        scratch_shapes=[
            pltpu.VMEM((CH + 16, ROWS * COLS), bf16),
            pltpu.VMEM((7, 1, CH, COLS), bf16),
            pltpu.VMEM((7, 1, CH, COLS), bf16),
            pltpu.VMEM((2, CH, 2 * COLS), bf16),
            pltpu.VMEM((2, CH, 2 * COLS), bf16),
            pltpu.VMEM((HALF, EXT * COLS), f32),
            pltpu.VMEM((9, HALF, 128), f32),
            pltpu.SemaphoreType.DMA((5,)),
        ],
        out_shape=[
            held((CH, ROWS * COLS), bf16),
            held((HALF, EXT * COLS), bf16),
            held((HALF, ROWS * COLS), bf16),
            held((HALF, ROWS * COLS), bf16),
            held((HALF, (ROWS + 2) * COLS), bf16),
            held((HALF, (ROWS + 2) * COLS), bf16),
            held((CH, HALF), f32),
            held((CH, HALF), bf16),
            held((CH, HALF), bf16),
            held((2, 8, 2, 16, 128), bf16),
            jax.ShapeDtypeStruct((16, 8, 128), f32),
        ],
        compiler_params=params(),
        cost_estimate=cost(10**9, 50 * 10**6),
        name="forward",
    )(weights, *far_memory(normed, near, far, own_c, other_c))


def excite_kernel(sums, own_rows, other_rows, coef):
    low = lanes_of((SQ, 128)) < 64
    totals = []
    for half in range(2):
        total = sums[half]
        for other in range(1, 8):
            total = total + sums[2 * other + half]
        totals.append(total)
    core, _ = tensor_place()
    is_first = core == 0
    ordered = (
        jnp.where(is_first, totals[0], totals[1]),
        jnp.where(is_first, totals[1], totals[0]),
    )
    pooled, grad_gate, down, up = [], [], [], []
    for total, rows in zip(ordered, (own_rows, other_rows)):
        for block in range(BLOCKS):
            pooled.append(total[block : block + 1] * (1.0 / CELLS))
            grad_gate.append(total[BLOCKS + block : BLOCKS + block + 1])
            halves = [
                jnp.concatenate(
                    [rows[yh, 2 * block + j, part].astype(f32) for yh in range(2) for part in range(2)],
                    axis=0,
                )
                for j in range(2)
            ]
            down.append(join_low(halves[0], halves[1], low))
            up.append(join_high(halves[0], halves[1], low))
    count = 2 * BLOCKS
    squeeze = sum(jnp.sum(down[b] * pooled[b], axis=1, keepdims=True) for b in range(count))
    sig = 1.0 / (1.0 + jnp.exp(-squeeze))
    swish = squeeze * sig
    gating, grad_excite = [], []
    for b in range(count):
        logit = jnp.sum(up[b] * swish, axis=0, keepdims=True)
        gating.append(1.0 / (1.0 + jnp.exp(-logit)))
        grad_excite.append(grad_gate[b] * gating[b] * (1.0 - gating[b]))
    grad_swish = sum(jnp.sum(up[b] * grad_excite[b], axis=1, keepdims=True) for b in range(count))
    grad_squeeze = grad_swish * sig * (1.0 + squeeze * (1.0 - sig))
    side = jnp.concatenate([swish, grad_squeeze], axis=0)
    side_row = jnp.broadcast_to(side, (128, 128)).T[0:1, :]
    for b in range(BLOCKS):
        cells = slice(b * 128, b * 128 + 128)
        grad_pooled = jnp.sum(down[b] * grad_squeeze, axis=0, keepdims=True)
        coef[0:1, cells] = gating[b]
        coef[1:2, cells] = grad_pooled * (1.0 / CELLS)
        coef[2:3, cells] = pooled[b]
        coef[3:4, cells] = grad_excite[b]
        coef[4:5, cells] = side_row
    coef[5:8, :] = jnp.zeros((3, HALF), f32)


def excite(sums, own_rows, other_rows):
    return pl.pallas_call(
        excite_kernel,
        in_specs=in_vmem(3),
        out_specs=in_vmem(1)[0],
        out_shape=held((8, HALF), f32),
        compiler_params=params(),
        cost_estimate=cost(SMALL, 4 * 10**6),
        name="excite",
    )(sums, *kept(own_rows), other_rows)


def backward_kernel(
    coef, weights, normed, act1, slope1, slope2, grad_hidden, proj_grad, w_proj, w_exp, act2,
    grad_out, pieces_out, other_out,
    grad_expanded, pieces, other, copied, pieces_copied, other_copied,
    taps, gates, pools, kernel_sums, tap_rows,
):
    for block in range(BLOCKS):
        cells = slice(block * 128, block * 128 + 128)
        spread_taps(
            [[weights[yh, 2 * block + j, 10] for j in range(2)] for yh in range(2)],
            taps,
            block * 128,
            True,
            0.5,
        )
        gates[cells, :] = down_rows(coef[0:1, cells] * 0.5)
        pools[cells, :] = down_rows(coef[1:2, cells] * 0.5)
    core, _ = tensor_place()
    cells = pl.ds(pl.multiple_of((1 - core) * (7 * COLS), 7 * COLS), 7 * COLS)
    gated = (w_proj[...].astype(f32) * (coef[0:1, :] * (0.5 / stretch))).astype(bf16)
    projected = jnp.dot(gated, act2[:, cells], preferred_element_type=f32).astype(bf16)
    for row in range(7):
        other[0, row] = projected[:, row * 128 : row * 128 + 128]
    other_copies = [
        pltpu.make_async_copy(other.at[i], other_out.at[i], other_copied.at[i]) for i in range(2)
    ]
    other_copies[0].start()
    lane = lanes_of((GROUP, COLS))

    def one_group(index, carry):
        rows = pl.ds(pl.multiple_of(index * GROUP, GROUP), GROUP)
        tap = [taps[k, rows, :] for k in range(9)]
        gating = gates[rows, :]
        pooled = pools[rows, :]
        running = {}
        acts = {}
        sums = [None] * 9
        for m in range(1, ROWS + 3):
            cells = slice((m - 1) * 128, m * 128)
            grad = grad_hidden[rows, cells].astype(f32) * gating + pooled
            grad = grad * slope2[rows, cells].astype(f32)
            turned = (pltpu.roll(grad, 127, 1), grad, pltpu.roll(grad, 1, 1))
            for h in ((1, 2) if m == 1 else (m + 1,)):
                if h <= ROWS + 2:
                    acts[h] = act1[rows, h * 128 : h * 128 + 128].astype(f32)
            for i in range(3):
                h = m + i - 1
                if 2 <= h < ROWS + 2:
                    term = tap[3 * i] * turned[0] + tap[3 * i + 1] * turned[1] + tap[3 * i + 2] * turned[2]
                    running[h] = running[h] + term if h in running else term
                if 2 <= m < ROWS + 2:
                    for j in range(3):
                        term = turned[j] * acts[h]
                        k = 3 * i + j
                        sums[k] = term if sums[k] is None else sums[k] + term
            h = m - 1
            if 2 <= h < ROWS + 2:
                out = slice((h - 2) * 128, (h - 1) * 128)
                grad_expanded[rows, out] = (running.pop(h) * slope1[rows, out].astype(f32)).astype(bf16)
        for k in range(9):
            total = sums[k] * 0.5
            if k % 3 == 0:
                total = jnp.where(lane == 127, 0.0, total)
            if k % 3 == 2:
                total = jnp.where(lane == 0, 0.0, total)
            kernel_sums[k, rows, :] = total
        return carry

    def block_copy(block):
        rows = pl.ds(pl.multiple_of(block * 128, 128), 128)
        return pltpu.make_async_copy(grad_expanded.at[rows], grad_out.at[rows], copied.at[block])

    def one_block(block, carry):
        first = block * (128 // GROUP)
        lax.fori_loop(0, 128 // GROUP, lambda i, c: one_group(first + i, c), 0, unroll=2)
        block_copy(block).start()
        return carry

    lax.fori_loop(0, BLOCKS, one_block, 0)
    grad = jnp.dot(w_exp[...], grad_expanded[:, cells], preferred_element_type=f32).astype(bf16)
    for row in range(7):
        other[1, row] = grad[:, row * 128 : row * 128 + 128]
    other_copies[1].start()
    exp_grad = lax.dot_general(
        normed[...], grad_expanded[...], (((1,), (1,)), ((), ())), preferred_element_type=f32
    )
    low = lanes_of((CH, 128)) < 64
    tap_low = lanes_of((1, 128)) < 64
    tap_rows[...] = jnp.zeros((16, 128), f32)

    def pieces_copy(block):
        part = pl.ds(2 * block, 2)
        return pltpu.make_async_copy(
            pieces.at[:, part], pieces_out.at[:, part], pieces_copied.at[block]
        )

    for block in range(BLOCKS):
        cells = slice(block * 128, block * 128 + 128)
        scaled = proj_grad[:, cells] * (coef[0:1, cells] * (0.5 / stretch))
        first = join_low(exp_grad[:, cells], scaled, low).astype(bf16)
        second = join_high(exp_grad[:, cells], scaled, low).astype(bf16)
        for k in range(9):
            tap_rows[k : k + 1, :] = jnp.sum(kernel_sums[k, cells, :].T, axis=0, keepdims=True)
        tap_rows[9:10, :] = join_low(coef[2:3, cells], coef[3:4, cells], tap_low)
        tap_rows[10:11, :] = coef[4:5, cells]
        first_taps = tap_rows[...].astype(bf16)
        tap_rows[0:9, :] = pltpu.roll(tap_rows[...], 64, 1)[0:9]
        tap_rows[9:10, :] = join_high(coef[2:3, cells], coef[3:4, cells], tap_low)
        second_taps = tap_rows[...].astype(bf16)
        for yh in range(2):
            for z in range(8):
                rows = slice((z * 2 + yh) * 16, (z * 2 + yh) * 16 + 16)
                pieces[yh, 2 * block, z] = first[rows]
                pieces[yh, 2 * block + 1, z] = second[rows]
            pieces[yh, 2 * block, 8] = first_taps
            pieces[yh, 2 * block + 1, 8] = second_taps
        pieces_copy(block).start()
    for block in range(BLOCKS):
        block_copy(block).wait()
        pieces_copy(block).wait()
    for copy in other_copies:
        copy.wait()


def backward(coef, weights, normed, act1, slope1, slope2, grad_hidden, proj_grad, w_proj, w_exp, act2):
    return pl.pallas_call(
        backward_kernel,
        in_specs=in_vmem(11),
        out_specs=in_hbm(3),
        scratch_shapes=[
            pltpu.VMEM((HALF, ROWS * COLS), bf16),
            pltpu.VMEM((2, 8, 9, 16, 128), bf16),
            pltpu.VMEM((2, 7, CH, COLS), bf16),
            pltpu.SemaphoreType.DMA((BLOCKS,)),
            pltpu.SemaphoreType.DMA((BLOCKS,)),
            pltpu.SemaphoreType.DMA((2,)),
            pltpu.VMEM((9, HALF, 128), f32),
            pltpu.VMEM((HALF, 128), f32),
            pltpu.VMEM((HALF, 128), f32),
            pltpu.VMEM((9, HALF, 128), f32),
            pltpu.VMEM((16, 128), f32),
        ],
        out_shape=[
            pltpu.HBM((HALF, ROWS * COLS), bf16),
            pltpu.HBM((2, 8, 9, 16, 128), bf16),
            pltpu.HBM((2, 7, CH, COLS), bf16),
        ],
        compiler_params=params(),
        cost_estimate=cost(10**9, 45 * 10**6),
        name="backward",
    )(
        *kept(
            coef, weights, normed, act1, slope1, slope2, grad_hidden, proj_grad, w_proj, w_exp, act2
        )
    )


def finish_kernel(coef, w_proj, w_exp, act2, grad_expanded, arrived, x, c, block_out, input_grad, done):
    core, _ = tensor_place()
    cells = pl.ds(pl.multiple_of(core * (7 * COLS), 7 * COLS), 7 * COLS)
    gated = (w_proj[...].astype(f32) * (coef[0:1, :] * (0.5 / stretch))).astype(bf16)
    done[...] = jnp.zeros((8, 128), f32)
    all_projected = jnp.dot(gated, act2[:, cells], preferred_element_type=f32)
    all_grad = jnp.dot(w_exp[...], grad_expanded[:, cells], preferred_element_type=f32)
    for row in range(7):
        projected = all_projected[:, row * 128 : row * 128 + 128] + arrived[0, row].astype(f32)
        values = x[row, 0].astype(f32)
        block_out[row, 0] = (values + projected).astype(bf16)
        grad = all_grad[:, row * 128 : row * 128 + 128] + arrived[1, row].astype(f32)
        center = values - jnp.mean(values, axis=0, keepdims=True)
        inv_std = lax.rsqrt(jnp.mean(center * center, axis=0, keepdims=True) + 1e-05)
        normal = center * inv_std
        mean_grad = jnp.mean(grad, axis=0, keepdims=True)
        mean_inner = jnp.mean(grad * normal, axis=0, keepdims=True)
        input_grad[row, 0] = (
            c[row, 0].astype(f32) + inv_std * (grad - mean_grad - normal * mean_inner)
        ).astype(bf16)


def finish(coef, w_proj, w_exp, act2, grad_expanded, arrived, x, c):
    return pl.pallas_call(
        finish_kernel,
        in_specs=in_vmem(8),
        out_specs=in_vmem(3),
        out_shape=[
            jax.ShapeDtypeStruct((7, 1, CH, COLS), bf16),
            jax.ShapeDtypeStruct((7, 1, CH, COLS), bf16),
            jax.ShapeDtypeStruct((8, 128), f32),
        ],
        compiler_params=params(),
        cost_estimate=cost(SMALL, SMALL),
        name="finish",
    )(*kept(coef, w_proj, w_exp, act2), grad_expanded, arrived, x, c)


def middle_kernel(pieces, after, out):
    for slot in range(9):
        total = pieces[0, slot].astype(f32)
        for other in range(1, 16):
            total = total + pieces[other, slot].astype(f32)
        total = total.astype(bf16)
        if slot < 8:
            out[slot, 0] = total
        else:
            for z in range(8):
                out[z, 1] = total
    low = lanes_of((SQ, 128)) < 64
    outer = jnp.zeros((SQ, 128), f32)
    for yh in range(2):
        vectors = pieces[yh * 8, 8].astype(f32)
        column = down_rows(vectors[10:11, :])
        outer = outer + jnp.where(low, column[64:128], column[0:64]) * vectors[9:10, :]
    outer = outer.astype(bf16)
    for z in range(8):
        for part in range(4):
            out[z, 2 + part] = outer[part * 16 : part * 16 + 16]


def middle(pieces, after):
    return pl.pallas_call(
        middle_kernel,
        in_specs=in_vmem(2),
        out_specs=in_vmem(1)[0],
        out_shape=jax.ShapeDtypeStruct((8, 6, 16, 128), bf16),
        compiler_params=params(),
        cost_estimate=cost(10**6, 4 * 10**6),
        name="middle",
    )(pieces, after)


def tail_kernel(lines, exp_grad, proj_grad, kernel_grad, down_grad, up_grad):
    def total_of(slot):
        total = lines[0, slot].astype(f32)
        for z in range(1, 8):
            total = total + lines[z, slot].astype(f32)
        return total

    first = total_of(0)
    exp_grad[...] = first[:, 0:64]
    proj_grad[...] = pltpu.roll(first, 64, 1)[:, 0:64]
    kernel_grad[...] = total_of(1)[0:9, 0:64]
    for part in range(4):
        both = total_of(2 + part)
        down_grad[part * 16 : part * 16 + 16, :] = both[:, 0:64]
        up_grad[part * 16 : part * 16 + 16, :] = pltpu.roll(both, 64, 1)[:, 0:64]


def tail(lines):
    return pl.pallas_call(
        tail_kernel,
        in_specs=in_vmem(1),
        out_specs=in_vmem(5),
        out_shape=[
            jax.ShapeDtypeStruct((16, 64), f32),
            jax.ShapeDtypeStruct((16, 64), f32),
            jax.ShapeDtypeStruct((9, 64), f32),
            jax.ShapeDtypeStruct((64, 64), f32),
            jax.ShapeDtypeStruct((64, 64), f32),
        ],
        compiler_params=params(),
        cost_estimate=cost(10**6, 2 * 10**6),
        name="tail",
    )(lines)


def body(inputs, cotangent, w_expand, w_project, dw_kernel, se_down, se_up):
    swap = [(i, i ^ 1) for i in range(16)]
    edges = [(i, i + 1) for i in range(1, 14, 2)] + [(i + 1, i) for i in range(1, 14, 2)]
    packed, edge = start(inputs, cotangent, w_expand, w_project, dw_kernel.T, se_down, se_up)
    with jax.named_scope("rows"):
        near = lax.ppermute(edge, "tensor", edges)
        other_x = lax.ppermute(inputs, "tensor", swap)
        other_c = lax.ppermute(cotangent, "tensor", swap)
        normed, main_done = main_norm(inputs, other_x)
        near, edge_done = edge_norm(near, main_done)
        far = lax.ppermute(near, "tensor", swap)
    with jax.named_scope("weights"):
        lines = exchange(packed, "dp", DEPTH)
        copies = spread(lines, edge_done)
        weights = exchange(copies, BOTH, PLANE).reshape(2, 8, 11, 16, 128)
    (
        normed, act1, slope1, act2, slope2, grad_hidden, proj_grad, w_exp, w_proj, own_rows, sums
    ) = forward(weights, normed, near, far, cotangent, other_c)
    with jax.named_scope("sums"):
        other_rows = lax.ppermute(own_rows, "tensor", swap)
        all_sums = exchange(sums, "tensor")
    coef = excite(all_sums, own_rows, other_rows)
    grad_expanded, pieces, partial_out = backward(
        coef, weights, normed, act1, slope1, slope2, grad_hidden, proj_grad, w_proj, w_exp, act2
    )
    with jax.named_scope("finish"):
        arrived = lax.ppermute(partial_out, "tensor", swap)
        block_out, input_grad, done = finish(
            coef, w_proj, w_exp, act2, grad_expanded, arrived, inputs, cotangent
        )
    with jax.named_scope("gradients"):
        pieces = exchange(pieces.reshape(16, 9, 16, 128), BOTH, PLANE)
        lines = exchange(middle(pieces, done), "dp", DEPTH)
        exp_grad, proj_grad, kernel_grad, down_grad, up_grad = tail(lines)
    return (block_out, input_grad, exp_grad, proj_grad, kernel_grad.T, down_grad, up_grad)


def solution(mesh):
    placed = (
        P("tensor", "dp", None, None),
        P("tensor", "dp", None, None),
        P("dp", "tensor"),
        P("dp", "tensor"),
        P("tensor", None),
        P(None, "tensor"),
        P(None, "tensor"),
    )
    return jax.shard_map(
        body,
        mesh=mesh,
        in_specs=placed,
        out_specs=(
            P("tensor", "dp", None, None),
            P("tensor", "dp", None, None),
            P("dp", "tensor"),
            P("dp", "tensor"),
            P("tensor", None),
            P(None, "tensor"),
            P(None, "tensor"),
        ),
        check_vma=False,
    )
```

```python
import jax
import jax.numpy as jnp
from jax import lax
from jax.experimental import pallas as pl
from jax.experimental.pallas import tpu as pltpu
from jax.sharding import PartitionSpec as P

bf16 = jnp.bfloat16
f32 = jnp.float32

gelu_scale = 0.7978845608
gelu_cubic = 0.044715

CH = 256
HALF = 512
SQ = 64
COLS = 128
ROWS = 14
EXT = ROWS + 4
CELLS = 112 * 128
BLOCKS = 4
GROUP = 16
BOTH = ("dp", "tensor")
VMEM = 16 * 1024 * 1024
SMALL = 10**5


def groups(count, steps):
    seen, found = set(), []
    for first in range(count):
        if first in seen:
            continue
        members = [first]
        for step in steps:
            members = members + [member ^ step for member in members]
        members = sorted(members)
        seen.update(members)
        found.append(members)
    return found


def exchange(pieces, axes, steps=None):
    members = None
    if steps is not None:
        members = groups(256 if axes == BOTH else 16, steps)
    return lax.all_to_all(pieces, axes, 0, 0, tiled=True, axis_index_groups=members)


def to_all(piece, count):
    return jnp.broadcast_to(piece[None], (count,) + piece.shape)


PLANE = (2, 4, 8, 16)
DEPTH = (2, 4, 8)


def gelu_pair(values):
    square = values * values
    inner = values * (gelu_scale + (gelu_scale * gelu_cubic) * square)
    tanh_part = jnp.tanh(inner)
    above = 1.0 + tanh_part
    act = values * above
    slope = above + act * (1.0 - tanh_part) * (
        gelu_scale + (3.0 * gelu_scale * gelu_cubic) * square
    )
    return act, slope


stretch = (gelu_scale * gelu_cubic) ** (1.0 / 3.0)


def stretched_gelu_pair(values):
    base = values * values + gelu_scale / stretch
    tanh_part = jnp.tanh(values * base)
    above = 1.0 + tanh_part
    act = values * above
    slope = above + act * (1.0 - tanh_part) * (3.0 * base - 2.0 * gelu_scale / stretch)
    return act, slope


def params(**more):
    return pltpu.CompilerParams(vmem_limit_bytes=VMEM, **more)


def cost(flops, size):
    return pl.CostEstimate(flops=flops, bytes_accessed=size, transcendentals=0)


def join_low(first, second, low):
    return jnp.where(low, first, pltpu.roll(second, 64, 1))


def join_high(first, second, low):
    return jnp.where(low, pltpu.roll(first, 64, 1), second)


def full(*shape):
    return pl.BlockSpec(shape, lambda *unused: (0,) * len(shape))


def in_vmem(count):
    return [pl.BlockSpec(memory_space=pltpu.VMEM)] * count


def in_hbm(count):
    return [pl.BlockSpec(memory_space=pltpu.HBM)] * count


def held(shape, kind):
    return pltpu.VMEM(shape, kind)


def kept(*arrays):
    return [pltpu.with_memory_space_constraint(array, pltpu.VMEM) for array in arrays]


def far_memory(*arrays):
    return [pltpu.with_memory_space_constraint(array, pltpu.HBM) for array in arrays]


def tensor_place():
    place = lax.axis_index("tensor")
    return lax.rem(place, 2), lax.div(place, 2)


def image_place():
    image = lax.axis_index("dp")
    return lax.div(image, 2), lax.rem(image, 2)


def lanes_of(shape):
    return lax.broadcasted_iota(jnp.int32, shape, 1)


def down_rows(row):
    return jnp.broadcast_to(row, (128, 128)).T


def start_kernel(
    x, c, w_expand, w_project, dw_rows, se_down, se_up,
    packed, edge,
    tall, wide, expand_in, project_in, dw_in, down_in, up_in, sems,
):
    core, _ = tensor_place()
    z, yh = image_place()
    pairs = (
        (w_expand, expand_in),
        (w_project, project_in),
        (dw_rows, dw_in),
        (se_down, down_in),
        (se_up, up_in),
        (x.at[pl.ds(5 * core, 2)], edge.at[0]),
        (c.at[pl.ds(5 * core, 2)], edge.at[1]),
    )
    copies = [pltpu.make_async_copy(a, b, sems.at[i]) for i, (a, b) in enumerate(pairs)]
    for copy in copies:
        copy.start()
    wide[0:16, :] = jnp.zeros((16, 128), f32)
    for copy in copies[:5]:
        copy.wait()
    wide[0:9, 0:64] = dw_in[...].astype(f32)
    tall[0:64, 0:64] = down_in[...].astype(f32)
    tall[0:64, 64:128] = up_in[...].astype(f32)
    wide[16:32, 0:64] = expand_in[...].astype(f32)
    wide[16:32, 64:128] = project_in[...].astype(f32)
    squeeze_rows = tall[pl.ds(yh * 32 + z * 4, 4), :]
    tap_row = wide[pl.ds(yh * 8 + z, 1), :]
    tall[16:32, :] = jnp.zeros((16, 128), f32)
    tall[16:20, :] = squeeze_rows
    tall[20:21, :] = tap_row
    piece = jnp.concatenate([wide[16:32, :], tall[16:32, :]], axis=0).astype(bf16)
    for other in range(8):
        packed[other] = piece
    for copy in copies[5:]:
        copy.wait()


def start(x, c, w_expand, w_project, dw_rows, se_down, se_up):
    return pl.pallas_call(
        start_kernel,
        in_specs=in_hbm(7),
        out_specs=in_vmem(2),
        out_shape=[
            jax.ShapeDtypeStruct((8, 32, 128), bf16),
            held((2, 2, 1, CH, COLS), bf16),
        ],
        scratch_shapes=[
            pltpu.VMEM((64, 128), f32),
            pltpu.VMEM((32, 128), f32),
            pltpu.VMEM((16, 64), bf16),
            pltpu.VMEM((16, 64), bf16),
            pltpu.VMEM((9, 64), bf16),
            pltpu.VMEM((64, 64), bf16),
            pltpu.VMEM((64, 64), bf16),
            pltpu.SemaphoreType.DMA((7,)),
        ],
        compiler_params=params(),
        cost_estimate=cost(SMALL, SMALL),
        name="start",
    )(*far_memory(x, c, w_expand, w_project, dw_rows, se_down, se_up))


def spread_kernel(lines, after, out, squeeze_rows, tap_rows):
    tap_rows[...] = jnp.zeros((16, 128), f32)
    for z in range(8):
        small = lines[z, 16:32, :].astype(f32)
        squeeze_rows[z * 4 : z * 4 + 4, :] = small[0:4]
        tap_rows[z : z + 1, :] = small[4:5]
    squeeze_piece = squeeze_rows[...].astype(bf16)
    tap_piece = tap_rows[...].astype(bf16)
    for other in range(16):
        for z in range(8):
            out[other, z] = lines[z, 0:16, :]
        out[other, 8] = squeeze_piece[0:16]
        out[other, 9] = squeeze_piece[16:32]
        out[other, 10] = tap_piece


def spread(lines, after):
    return pl.pallas_call(
        spread_kernel,
        in_specs=in_vmem(2),
        out_specs=in_vmem(1)[0],
        out_shape=jax.ShapeDtypeStruct((16, 11, 16, 128), bf16),
        scratch_shapes=[pltpu.VMEM((32, 128), f32), pltpu.VMEM((16, 128), f32)],
        compiler_params=params(),
        cost_estimate=cost(SMALL, SMALL),
        name="spread",
    )(lines, after)


def normal_of(x):
    values = x.astype(f32)
    center = values - jnp.mean(values, axis=0, keepdims=True)
    inv_std = lax.rsqrt(jnp.mean(center * center, axis=0, keepdims=True) + 1e-05)
    return (center * inv_std).astype(bf16)


def lane_block(row):
    return pl.ds(pl.multiple_of(row * 128, 128), 128)


def copy_all(pairs, sems):
    copies = [pltpu.make_async_copy(a, b, sems.at[i]) for i, (a, b) in enumerate(pairs)]
    for copy in copies:
        copy.start()
    return copies


def main_norm_kernel(own_x, other_x, normed_out, done, own_x_in, other_x_in, normed, sems):
    done[...] = jnp.zeros((8, 128), f32)
    core, _ = tensor_place()
    copies = copy_all(((own_x, own_x_in), (other_x, other_x_in)), sems)
    sent = []
    for i, (x, first) in enumerate(((own_x_in, 7 * core), (other_x_in, 7 - 7 * core))):
        copies[i].wait()
        for row in range(7):
            normed[i, :, row * 128 : row * 128 + 128] = normal_of(x[row, 0])
        part = pl.ds(pl.multiple_of(first * 128, 7 * 128), 7 * 128)
        sent.append(pltpu.make_async_copy(normed.at[i], normed_out.at[:, part], sems.at[i]))
        sent[i].start()
    for copy in sent:
        copy.wait()


def main_norm(own_x, other_x):
    return pl.pallas_call(
        main_norm_kernel,
        in_specs=in_hbm(2),
        out_specs=in_hbm(1) + in_vmem(1),
        out_shape=[
            pltpu.HBM((CH, ROWS * COLS), bf16),
            jax.ShapeDtypeStruct((8, 128), f32),
        ],
        scratch_shapes=[pltpu.VMEM((7, 1, CH, COLS), bf16)] * 2
        + [pltpu.VMEM((2, CH, 7 * COLS), bf16), pltpu.SemaphoreType.DMA((2,))],
        compiler_params=params(),
        cost_estimate=cost(SMALL, SMALL),
        name="main_norm",
    )(*far_memory(own_x, other_x))


def edge_norm_kernel(near, after, edge_out, done, edge, sem):
    done[...] = after[...]
    for row in range(2):
        edge[0, :, row * 128 : row * 128 + 128] = normal_of(near[0, row, 0])
        edge[1, :, row * 128 : row * 128 + 128] = near[1, row, 0]
    copy = pltpu.make_async_copy(edge, edge_out, sem)
    copy.start()
    copy.wait()


def edge_norm(near, after):
    return pl.pallas_call(
        edge_norm_kernel,
        in_specs=in_vmem(2),
        out_specs=in_hbm(1) + in_vmem(1),
        out_shape=[pltpu.HBM((2, CH, 2 * COLS), bf16), jax.ShapeDtypeStruct((8, 128), f32)],
        scratch_shapes=[
            pltpu.VMEM((2, CH, 2 * COLS), bf16),
            pltpu.SemaphoreType.DMA,
        ],
        compiler_params=params(),
        cost_estimate=cost(SMALL, SMALL),
        name="edge_norm",
    )(near, after)


def spread_taps(sources, taps, place, turned, scale):
    low = lanes_of((16, 128)) < 64
    early = join_low(sources[0][0].astype(f32), sources[0][1].astype(f32), low)
    late = join_low(sources[1][0].astype(f32), sources[1][1].astype(f32), low)
    early = early * scale
    late = late * scale
    lane = lanes_of((128, 128))
    for tap in range(9):
        spread = down_rows(early[tap : tap + 1, :] if tap < 8 else late[0:1, :])
        if tap % 3 == (2 if turned else 0):
            spread = jnp.where(lane == 0, 0.0, spread)
        if tap % 3 == (0 if turned else 2):
            spread = jnp.where(lane == 127, 0.0, spread)
        taps[tap, place : place + 128, :] = spread


def forward_kernel(
    weights, normed_in, near_in, far_in, own_c, other_c,
    normed, act1, slope1, act2, slope2, grad_hidden, proj_grad, w_exp, w_proj, squeeze_rows, sums,
    cot, own_c_in, other_c_in, near, far, expanded, taps, sems,
):
    core, chip = tensor_place()
    copies = copy_all(
        (
            (normed_in, normed),
            (near_in, near),
            (far_in, far),
            (own_c, own_c_in),
            (other_c, other_c_in),
        ),
        sems,
    )
    low = lanes_of((16, 128)) < 64
    for block in range(BLOCKS):
        cells = slice(block * 128, block * 128 + 128)
        for z in range(8):
            for yh in range(2):
                first = weights[yh, 2 * block, z].astype(f32)
                second = weights[yh, 2 * block + 1, z].astype(f32)
                rows = slice((z * 2 + yh) * 16, (z * 2 + yh) * 16 + 16)
                w_exp[rows, cells] = join_low(first, second, low).astype(bf16)
                w_proj[rows, cells] = join_high(first, second, low).astype(bf16)
        spread_taps(
            [[weights[yh, 2 * block + j, 10] for j in range(2)] for yh in range(2)],
            taps,
            block * 128,
            False,
            0.5 * stretch,
        )
    squeeze_rows[...] = weights[:, :, 8:10]

    def multiply(weight, source, target, place):
        target[:, place * 128 : place * 128 + source.shape[1]] = lax.dot_general(
            weight[...], source, (((0,), (0,)), ((), ())), preferred_element_type=f32
        ).astype(target.dtype)

    copies[0].wait()
    for part in range(ROWS // 2):
        cells = slice(part * 256, part * 256 + 256)
        multiply(w_exp, normed[:, cells], expanded, 2 + 2 * part)
    for copy in copies[1:3]:
        copy.wait()
    near_first = core == 0
    multiply(w_exp, jnp.where(near_first, near[0], far[0]), expanded, 0)
    multiply(w_exp, jnp.where(near_first, far[0], near[0]), expanded, ROWS + 2)
    first_chip = jnp.where(chip > 0, 1.0, 0.0)
    last_chip = jnp.where(chip < 7, 1.0, 0.0)

    def one_group(index, carry):
        rows = pl.ds(pl.multiple_of(index * GROUP, GROUP), GROUP)
        tap = [taps[k, rows, :] for k in range(9)]
        running = {}
        for h in range(EXT):
            act, slope = gelu_pair(expanded[rows, h * 128 : h * 128 + 128])
            act1[rows, h * 128 : h * 128 + 128] = act.astype(bf16)
            if 2 <= h < ROWS + 2:
                slope1[rows, (h - 2) * 128 : (h - 1) * 128] = slope.astype(bf16)
            left = pltpu.roll(act, 1, 1)
            right = pltpu.roll(act, 127, 1)
            for i in range(3):
                m = h + 1 - i
                if not 1 <= m <= ROWS + 2:
                    continue
                term = tap[3 * i] * left + tap[3 * i + 1] * act + tap[3 * i + 2] * right
                running[m] = running[m] + term if m in running else term
            m = h - 1
            if not 1 <= m <= ROWS + 2:
                continue
            act, slope = stretched_gelu_pair(running.pop(m))
            if m == 1:
                slope = slope * first_chip
            if m == ROWS + 2:
                slope = slope * last_chip
            slope2[rows, (m - 1) * 128 : m * 128] = slope.astype(bf16)
            if 2 <= m < ROWS + 2:
                act2[rows, (m - 2) * 128 : (m - 1) * 128] = act.astype(bf16)
        return carry

    lax.fori_loop(0, HALF // GROUP, one_group, 0, unroll=2)
    cot[CH : CH + 16, :] = jnp.ones((16, ROWS * COLS), bf16)
    for copy, c, first in ((copies[3], own_c_in, 7 * core), (copies[4], other_c_in, 7 - 7 * core)):
        copy.wait()
        for row in range(7):
            cot[0:CH, lane_block(first + row)] = c[row, 0]
    products = lax.dot_general(
        cot[...], act2[...], (((1,), (1,)), ((), ())), preferred_element_type=f32
    )
    proj_grad[...] = products[0:CH]
    pool = products[CH : CH + 1] * (0.5 / stretch)
    gate = jnp.sum(products[0:CH] * w_proj[...].astype(f32), axis=0, keepdims=True)
    gate = gate * (0.5 / stretch)
    for other in range(16):
        for block in range(BLOCKS):
            cells = slice(block * 128, block * 128 + 128)
            sums[other, block : block + 1, :] = pool[:, cells]
            sums[other, BLOCKS + block : BLOCKS + block + 1, :] = gate[:, cells]
    above = jnp.where(near_first, near[1, :, 128:256], far[1, :, 128:256])
    below = jnp.where(near_first, far[1, :, 0:128], near[1, :, 0:128])
    multiply(w_proj, above, grad_hidden, 0)
    multiply(w_proj, below, grad_hidden, ROWS + 1)
    for part in range(ROWS // 2):
        cells = slice(part * 256, part * 256 + 256)
        multiply(w_proj, cot[0:CH, cells], grad_hidden, 1 + 2 * part)


def forward(weights, normed, near, far, own_c, other_c):
    return pl.pallas_call(
        forward_kernel,
        in_specs=in_vmem(1) + in_hbm(5),
        out_specs=in_vmem(11),
        scratch_shapes=[
            pltpu.VMEM((CH + 16, ROWS * COLS), bf16),
            pltpu.VMEM((7, 1, CH, COLS), bf16),
            pltpu.VMEM((7, 1, CH, COLS), bf16),
            pltpu.VMEM((2, CH, 2 * COLS), bf16),
            pltpu.VMEM((2, CH, 2 * COLS), bf16),
            pltpu.VMEM((HALF, EXT * COLS), f32),
            pltpu.VMEM((9, HALF, 128), f32),
            pltpu.SemaphoreType.DMA((5,)),
        ],
        out_shape=[
            held((CH, ROWS * COLS), bf16),
            held((HALF, EXT * COLS), bf16),
            held((HALF, ROWS * COLS), bf16),
            held((HALF, ROWS * COLS), bf16),
            held((HALF, (ROWS + 2) * COLS), bf16),
            held((HALF, (ROWS + 2) * COLS), bf16),
            held((CH, HALF), f32),
            held((CH, HALF), bf16),
            held((CH, HALF), bf16),
            held((2, 8, 2, 16, 128), bf16),
            jax.ShapeDtypeStruct((16, 8, 128), f32),
        ],
        compiler_params=params(),
        cost_estimate=cost(10**9, 50 * 10**6),
        name="forward",
    )(weights, *far_memory(normed, near, far, own_c, other_c))


def excite_kernel(sums, own_rows, other_rows, coef):
    low = lanes_of((SQ, 128)) < 64
    totals = []
    for half in range(2):
        total = sums[half]
        for other in range(1, 8):
            total = total + sums[2 * other + half]
        totals.append(total)
    core, _ = tensor_place()
    is_first = core == 0
    ordered = (
        jnp.where(is_first, totals[0], totals[1]),
        jnp.where(is_first, totals[1], totals[0]),
    )
    pooled, grad_gate, down, up = [], [], [], []
    for total, rows in zip(ordered, (own_rows, other_rows)):
        for block in range(BLOCKS):
            pooled.append(total[block : block + 1] * (1.0 / CELLS))
            grad_gate.append(total[BLOCKS + block : BLOCKS + block + 1])
            halves = [
                jnp.concatenate(
                    [rows[yh, 2 * block + j, part].astype(f32) for yh in range(2) for part in range(2)],
                    axis=0,
                )
                for j in range(2)
            ]
            down.append(join_low(halves[0], halves[1], low))
            up.append(join_high(halves[0], halves[1], low))
    count = 2 * BLOCKS
    squeeze = sum(jnp.sum(down[b] * pooled[b], axis=1, keepdims=True) for b in range(count))
    sig = 1.0 / (1.0 + jnp.exp(-squeeze))
    swish = squeeze * sig
    gating, grad_excite = [], []
    for b in range(count):
        logit = jnp.sum(up[b] * swish, axis=0, keepdims=True)
        gating.append(1.0 / (1.0 + jnp.exp(-logit)))
        grad_excite.append(grad_gate[b] * gating[b] * (1.0 - gating[b]))
    grad_swish = sum(jnp.sum(up[b] * grad_excite[b], axis=1, keepdims=True) for b in range(count))
    grad_squeeze = grad_swish * sig * (1.0 + squeeze * (1.0 - sig))
    side = jnp.concatenate([swish, grad_squeeze], axis=0)
    side_row = jnp.broadcast_to(side, (128, 128)).T[0:1, :]
    for b in range(BLOCKS):
        cells = slice(b * 128, b * 128 + 128)
        grad_pooled = jnp.sum(down[b] * grad_squeeze, axis=0, keepdims=True)
        coef[0:1, cells] = gating[b]
        coef[1:2, cells] = grad_pooled * (1.0 / CELLS)
        coef[2:3, cells] = pooled[b]
        coef[3:4, cells] = grad_excite[b]
        coef[4:5, cells] = side_row
    coef[5:8, :] = jnp.zeros((3, HALF), f32)


def backward_kernel(
    all_sums, own_rows, other_rows,
    weights, normed, act1, slope1, slope2, grad_hidden, proj_grad, w_proj, w_exp, act2,
    coef, grad_out, pieces_out, other_out,
    grad_expanded, pieces, other, copied, pieces_copied, other_copied,
    taps, gates, pools, kernel_sums, tap_rows,
):
    excite_kernel(all_sums, own_rows, other_rows, coef)
    for block in range(BLOCKS):
        cells = slice(block * 128, block * 128 + 128)
        spread_taps(
            [[weights[yh, 2 * block + j, 10] for j in range(2)] for yh in range(2)],
            taps,
            block * 128,
            True,
            0.5,
        )
        gates[cells, :] = down_rows(coef[0:1, cells] * 0.5)
        pools[cells, :] = down_rows(coef[1:2, cells] * 0.5)
    core, _ = tensor_place()
    cells = pl.ds(pl.multiple_of((1 - core) * (7 * COLS), 7 * COLS), 7 * COLS)
    gated = (w_proj[...].astype(f32) * (coef[0:1, :] * (0.5 / stretch))).astype(bf16)
    projected = jnp.dot(gated, act2[:, cells], preferred_element_type=f32).astype(bf16)
    for row in range(7):
        other[0, row] = projected[:, row * 128 : row * 128 + 128]
    other_copies = [
        pltpu.make_async_copy(other.at[i], other_out.at[i], other_copied.at[i]) for i in range(2)
    ]
    other_copies[0].start()
    lane = lanes_of((GROUP, COLS))

    def one_group(index, carry):
        rows = pl.ds(pl.multiple_of(index * GROUP, GROUP), GROUP)
        tap = [taps[k, rows, :] for k in range(9)]
        gating = gates[rows, :]
        pooled = pools[rows, :]
        running = {}
        acts = {}
        sums = [None] * 9
        for m in range(1, ROWS + 3):
            cells = slice((m - 1) * 128, m * 128)
            grad = grad_hidden[rows, cells].astype(f32) * gating + pooled
            grad = grad * slope2[rows, cells].astype(f32)
            turned = (pltpu.roll(grad, 127, 1), grad, pltpu.roll(grad, 1, 1))
            for h in ((1, 2) if m == 1 else (m + 1,)):
                if h <= ROWS + 2:
                    acts[h] = act1[rows, h * 128 : h * 128 + 128].astype(f32)
            for i in range(3):
                h = m + i - 1
                if 2 <= h < ROWS + 2:
                    term = tap[3 * i] * turned[0] + tap[3 * i + 1] * turned[1] + tap[3 * i + 2] * turned[2]
                    running[h] = running[h] + term if h in running else term
                if 2 <= m < ROWS + 2:
                    for j in range(3):
                        term = turned[j] * acts[h]
                        k = 3 * i + j
                        sums[k] = term if sums[k] is None else sums[k] + term
            h = m - 1
            if 2 <= h < ROWS + 2:
                out = slice((h - 2) * 128, (h - 1) * 128)
                grad_expanded[rows, out] = (running.pop(h) * slope1[rows, out].astype(f32)).astype(bf16)
        for k in range(9):
            total = sums[k] * 0.5
            if k % 3 == 0:
                total = jnp.where(lane == 127, 0.0, total)
            if k % 3 == 2:
                total = jnp.where(lane == 0, 0.0, total)
            kernel_sums[k, rows, :] = total
        return carry

    def block_copy(block):
        rows = pl.ds(pl.multiple_of(block * 128, 128), 128)
        return pltpu.make_async_copy(grad_expanded.at[rows], grad_out.at[rows], copied.at[block])

    def one_block(block, carry):
        first = block * (128 // GROUP)
        lax.fori_loop(0, 128 // GROUP, lambda i, c: one_group(first + i, c), 0, unroll=4)
        block_copy(block).start()
        return carry

    lax.fori_loop(0, BLOCKS, one_block, 0)
    grad = jnp.dot(w_exp[...], grad_expanded[:, cells], preferred_element_type=f32).astype(bf16)
    for row in range(7):
        other[1, row] = grad[:, row * 128 : row * 128 + 128]
    other_copies[1].start()
    exp_grad = lax.dot_general(
        normed[...], grad_expanded[...], (((1,), (1,)), ((), ())), preferred_element_type=f32
    )
    low = lanes_of((CH, 128)) < 64
    tap_low = lanes_of((1, 128)) < 64
    tap_rows[...] = jnp.zeros((16, 128), f32)

    def pieces_copy(block):
        part = pl.ds(2 * block, 2)
        return pltpu.make_async_copy(
            pieces.at[:, part], pieces_out.at[:, part], pieces_copied.at[block]
        )

    for block in range(BLOCKS):
        cells = slice(block * 128, block * 128 + 128)
        scaled = proj_grad[:, cells] * (coef[0:1, cells] * (0.5 / stretch))
        first = join_low(exp_grad[:, cells], scaled, low).astype(bf16)
        second = join_high(exp_grad[:, cells], scaled, low).astype(bf16)
        for k in range(9):
            tap_rows[k : k + 1, :] = jnp.sum(kernel_sums[k, cells, :].T, axis=0, keepdims=True)
        tap_rows[9:10, :] = join_low(coef[2:3, cells], coef[3:4, cells], tap_low)
        tap_rows[10:11, :] = coef[4:5, cells]
        first_taps = tap_rows[...].astype(bf16)
        tap_rows[0:9, :] = pltpu.roll(tap_rows[...], 64, 1)[0:9]
        tap_rows[9:10, :] = join_high(coef[2:3, cells], coef[3:4, cells], tap_low)
        second_taps = tap_rows[...].astype(bf16)
        for yh in range(2):
            for z in range(8):
                rows = slice((z * 2 + yh) * 16, (z * 2 + yh) * 16 + 16)
                pieces[yh, 2 * block, z] = first[rows]
                pieces[yh, 2 * block + 1, z] = second[rows]
            pieces[yh, 2 * block, 8] = first_taps
            pieces[yh, 2 * block + 1, 8] = second_taps
        pieces_copy(block).start()
    for block in range(BLOCKS):
        block_copy(block).wait()
        pieces_copy(block).wait()
    for copy in other_copies:
        copy.wait()


def backward(all_sums, own_rows, other_rows, weights, normed, act1, slope1, slope2, grad_hidden, proj_grad, w_proj, w_exp, act2):
    return pl.pallas_call(
        backward_kernel,
        in_specs=in_vmem(13),
        out_specs=in_vmem(1) + in_hbm(3),
        scratch_shapes=[
            pltpu.VMEM((HALF, ROWS * COLS), bf16),
            pltpu.VMEM((2, 8, 9, 16, 128), bf16),
            pltpu.VMEM((2, 7, CH, COLS), bf16),
            pltpu.SemaphoreType.DMA((BLOCKS,)),
            pltpu.SemaphoreType.DMA((BLOCKS,)),
            pltpu.SemaphoreType.DMA((2,)),
            pltpu.VMEM((9, HALF, 128), f32),
            pltpu.VMEM((HALF, 128), f32),
            pltpu.VMEM((HALF, 128), f32),
            pltpu.VMEM((9, HALF, 128), f32),
            pltpu.VMEM((16, 128), f32),
        ],
        out_shape=[
            held((8, HALF), f32),
            pltpu.HBM((HALF, ROWS * COLS), bf16),
            pltpu.HBM((2, 8, 9, 16, 128), bf16),
            pltpu.HBM((2, 7, CH, COLS), bf16),
        ],
        compiler_params=params(),
        cost_estimate=cost(10**9, 45 * 10**6),
        name="backward",
    )(
        all_sums,
        *kept(own_rows),
        other_rows,
        *kept(
            weights, normed, act1, slope1, slope2, grad_hidden, proj_grad, w_proj, w_exp, act2
        )
    )


def finish_kernel(coef, w_proj, w_exp, act2, grad_expanded, arrived, x, c, block_out, input_grad, done):
    core, _ = tensor_place()
    cells = pl.ds(pl.multiple_of(core * (7 * COLS), 7 * COLS), 7 * COLS)
    gated = (w_proj[...].astype(f32) * (coef[0:1, :] * (0.5 / stretch))).astype(bf16)
    done[...] = jnp.zeros((8, 128), f32)
    all_projected = jnp.dot(gated, act2[:, cells], preferred_element_type=f32)
    all_grad = jnp.dot(w_exp[...], grad_expanded[:, cells], preferred_element_type=f32)
    for row in range(7):
        projected = all_projected[:, row * 128 : row * 128 + 128] + arrived[0, row].astype(f32)
        values = x[row, 0].astype(f32)
        block_out[row, 0] = (values + projected).astype(bf16)
        grad = all_grad[:, row * 128 : row * 128 + 128] + arrived[1, row].astype(f32)
        center = values - jnp.mean(values, axis=0, keepdims=True)
        inv_std = lax.rsqrt(jnp.mean(center * center, axis=0, keepdims=True) + 1e-05)
        normal = center * inv_std
        mean_grad = jnp.mean(grad, axis=0, keepdims=True)
        mean_inner = jnp.mean(grad * normal, axis=0, keepdims=True)
        input_grad[row, 0] = (
            c[row, 0].astype(f32) + inv_std * (grad - mean_grad - normal * mean_inner)
        ).astype(bf16)


def finish(coef, w_proj, w_exp, act2, grad_expanded, arrived, x, c):
    return pl.pallas_call(
        finish_kernel,
        in_specs=in_vmem(8),
        out_specs=in_vmem(3),
        out_shape=[
            jax.ShapeDtypeStruct((7, 1, CH, COLS), bf16),
            jax.ShapeDtypeStruct((7, 1, CH, COLS), bf16),
            jax.ShapeDtypeStruct((8, 128), f32),
        ],
        compiler_params=params(),
        cost_estimate=cost(SMALL, SMALL),
        name="finish",
    )(*kept(coef, w_proj, w_exp, act2), grad_expanded, arrived, x, c)


def middle_kernel(pieces, after, out):
    for slot in range(9):
        total = pieces[0, slot].astype(f32)
        for other in range(1, 16):
            total = total + pieces[other, slot].astype(f32)
        total = total.astype(bf16)
        if slot < 8:
            out[slot, 0] = total
        else:
            for z in range(8):
                out[z, 1] = total
    low = lanes_of((SQ, 128)) < 64
    outer = jnp.zeros((SQ, 128), f32)
    for yh in range(2):
        vectors = pieces[yh * 8, 8].astype(f32)
        column = down_rows(vectors[10:11, :])
        outer = outer + jnp.where(low, column[64:128], column[0:64]) * vectors[9:10, :]
    outer = outer.astype(bf16)
    for z in range(8):
        for part in range(4):
            out[z, 2 + part] = outer[part * 16 : part * 16 + 16]


def middle(pieces, after):
    return pl.pallas_call(
        middle_kernel,
        in_specs=in_vmem(2),
        out_specs=in_vmem(1)[0],
        out_shape=jax.ShapeDtypeStruct((8, 6, 16, 128), bf16),
        compiler_params=params(),
        cost_estimate=cost(10**6, 4 * 10**6),
        name="middle",
    )(pieces, after)


def tail_kernel(lines, exp_grad, proj_grad, kernel_grad, down_grad, up_grad):
    def total_of(slot):
        total = lines[0, slot].astype(f32)
        for z in range(1, 8):
            total = total + lines[z, slot].astype(f32)
        return total

    first = total_of(0)
    exp_grad[...] = first[:, 0:64]
    proj_grad[...] = pltpu.roll(first, 64, 1)[:, 0:64]
    kernel_grad[...] = total_of(1)[0:9, 0:64]
    for part in range(4):
        both = total_of(2 + part)
        down_grad[part * 16 : part * 16 + 16, :] = both[:, 0:64]
        up_grad[part * 16 : part * 16 + 16, :] = pltpu.roll(both, 64, 1)[:, 0:64]


def tail(lines):
    return pl.pallas_call(
        tail_kernel,
        in_specs=in_vmem(1),
        out_specs=in_vmem(5),
        out_shape=[
            jax.ShapeDtypeStruct((16, 64), f32),
            jax.ShapeDtypeStruct((16, 64), f32),
            jax.ShapeDtypeStruct((9, 64), f32),
            jax.ShapeDtypeStruct((64, 64), f32),
            jax.ShapeDtypeStruct((64, 64), f32),
        ],
        compiler_params=params(),
        cost_estimate=cost(10**6, 2 * 10**6),
        name="tail",
    )(lines)


def body(inputs, cotangent, w_expand, w_project, dw_kernel, se_down, se_up):
    swap = [(i, i ^ 1) for i in range(16)]
    edges = [(i, i + 1) for i in range(1, 14, 2)] + [(i + 1, i) for i in range(1, 14, 2)]
    packed, edge = start(inputs, cotangent, w_expand, w_project, dw_kernel.T, se_down, se_up)
    with jax.named_scope("rows"):
        near = lax.ppermute(edge, "tensor", edges)
        other_x = lax.ppermute(inputs, "tensor", swap)
        other_c = lax.ppermute(cotangent, "tensor", swap)
        normed, main_done = main_norm(inputs, other_x)
        near, edge_done = edge_norm(near, main_done)
        far = lax.ppermute(near, "tensor", swap)
    with jax.named_scope("weights"):
        lines = exchange(packed, "dp", DEPTH)
        copies = spread(lines, edge_done)
        weights = exchange(copies, BOTH, PLANE).reshape(2, 8, 11, 16, 128)
    (
        normed, act1, slope1, act2, slope2, grad_hidden, proj_grad, w_exp, w_proj, own_rows, sums
    ) = forward(weights, normed, near, far, cotangent, other_c)
    with jax.named_scope("sums"):
        other_rows = lax.ppermute(own_rows, "tensor", swap)
        all_sums = exchange(sums, "tensor")
    coef, grad_expanded, pieces, partial_out = backward(
        all_sums, own_rows, other_rows, weights, normed, act1, slope1, slope2, grad_hidden, proj_grad, w_proj, w_exp, act2
    )
    with jax.named_scope("finish"):
        arrived = lax.ppermute(partial_out, "tensor", swap)
        block_out, input_grad, done = finish(
            coef, w_proj, w_exp, act2, grad_expanded, arrived, inputs, cotangent
        )
    with jax.named_scope("gradients"):
        pieces = exchange(pieces.reshape(16, 9, 16, 128), BOTH, PLANE)
        lines = exchange(middle(pieces, done), "dp", DEPTH)
        exp_grad, proj_grad, kernel_grad, down_grad, up_grad = tail(lines)
    return (block_out, input_grad, exp_grad, proj_grad, kernel_grad.T, down_grad, up_grad)


def solution(mesh):
    placed = (
        P("tensor", "dp", None, None),
        P("tensor", "dp", None, None),
        P("dp", "tensor"),
        P("dp", "tensor"),
        P("tensor", None),
        P(None, "tensor"),
        P(None, "tensor"),
    )
    return jax.shard_map(
        body,
        mesh=mesh,
        in_specs=placed,
        out_specs=(
            P("tensor", "dp", None, None),
            P("tensor", "dp", None, None),
            P("dp", "tensor"),
            P("dp", "tensor"),
            P("tensor", None),
            P(None, "tensor"),
            P(None, "tensor"),
        ),
        check_vma=False,
    )
```
